512 devices in a mesh: rows: 64 (over y, x, core), env: 8 (over z).
Axes of the slice: x: 4, y: 8, z: 8, core: 2. Of those that a mesh axis runs over, the one named last changes fastest.
Arguments:
- features: bfloat16 [16384, 1024], P('rows'), may hold values from -6 to 6
- environments: bfloat16 [2048, 1024], P('env'), may hold values from -0.1875 to 0.1875
- projector: bfloat16 [2048, 2048], P('env'), may hold values from -0.125 to 0.125
- metric: bfloat16 [512, 8, 32, 32], P('rows'), may hold values from -0.375 to 0.375
- neighbours: int32 [512, 8], P('rows'), may hold values from 0 to 511, as said below
- counts: int32 [512], P('rows'), may hold values from 16 to 32, as said below
- target: float32 [16384], P('rows'), may hold values from -6 to 6
Outputs:
- gram: float32 [2048, 2048], P('rows', 'env')
- rhs: float32 [2048], P('env')
The draws below stay inside these ranges and needn't reach their ends.
Inputs may be any that keep to these rules, and one draw needn't show every extreme that they name: `neighbours`: slot 0 is the block itself; every neighbour lies within 8 blocks of its block. `counts`: some block is full in every draw.
All inputs are finite; a program needn't handle non-finite values.
Results may differ from the reference program's by a relative error of at most 0.0067.
Values may be sent and summed in bfloat16 or wider, within the bound.
No kernel may reach another device: no remote copies, remote signals or barrier semaphores. Data moves between devices by JAX's collectives and lax.ppermute only.
A program may use at most 64 MiB of HBM per device.

```python
import jax
import jax.numpy as jnp
from jax import lax

FEAT = 1024
ENVS = 2048
BLK = 32
NNB = 8
NB_DEV = 8
NBLK = 512
ROWS = 16384


def draw_neighbours(key, part):
    key = jax.random.fold_in(key, 11)
    block = jnp.arange(NBLK, dtype=jnp.int32)[:, None]
    lower = jnp.maximum(block - NB_DEV, 0)
    upper = jnp.minimum(block + NB_DEV, NBLK - 1)
    raw = jax.random.randint(key, (NBLK, NNB), 0, 1 << 20, dtype=jnp.int32)
    picked = lower + raw % (upper - lower + 1)
    first = jnp.arange(NNB, dtype=jnp.int32)[None, :] == 0
    return jnp.where(first, block, picked).astype(jnp.int32)


def draw_counts(key, part):
    key = jax.random.fold_in(key, 23)
    first, second = jax.random.split(key)
    values = jax.random.randint(first, (NBLK,), BLK // 2, BLK + 1, dtype=jnp.int32)
    spot = jax.random.randint(second, (), 0, NBLK, dtype=jnp.int32)
    return jnp.where(jnp.arange(NBLK, dtype=jnp.int32) == spot, BLK, values).astype(jnp.int32)


def block_levels(own_key, dims, cuts, least, largest):
    factor_of, own = 1.0, jax.random.fold_in(own_key, 6)
    for dim, parts in cuts:
        steps = jnp.exp(jax.random.uniform(jax.random.fold_in(own, dim), (parts,), jnp.float32, least / len(cuts), largest / len(cuts)))
        factor_of = factor_of * jnp.repeat(steps, dims[dim] // parts).reshape([-1 if axis == dim else 1 for axis in range(len(dims))])
    return factor_of


def normal_values(own_key, extent, spread, most, shards=(), kind=jnp.bfloat16):
    values = jax.random.normal(own_key, extent, jnp.float32) * spread
    if len(shards) > 0:
        values = block_levels(own_key, extent, shards, -0.22, 0.18) * values
    return jnp.clip(values, min=-most, max=most).astype(kind)


def setup_inputs(seed: int = 0) -> dict:
    keys = jax.random.split(jax.random.key(seed), 8)
    features = normal_values(keys[0], (ROWS, FEAT), 1.0, 6.0, ((0, 64),))
    environments = normal_values(keys[1], (ENVS, FEAT), FEAT ** -0.5, 0.1875, ((0, 8),))
    projector = normal_values(keys[2], (ENVS, ENVS), ENVS ** -0.5, 0.125, ((0, 8),))
    metric = normal_values(keys[3], (NBLK, NNB, BLK, BLK), (NNB * BLK) ** -0.5, 0.375, ((0, 64),))
    neighbours = draw_neighbours(jax.random.fold_in(keys[7], 71), 0)
    counts = draw_counts(jax.random.fold_in(keys[7], 71), 0)
    target = normal_values(keys[6], (ROWS,), 1.0, 6.0, ((0, 64),), jnp.float32)
    return dict(features=features, environments=environments, projector=projector, metric=metric, neighbours=neighbours, counts=counts, target=target)


def reference(features, environments, projector, metric, neighbours, counts, target):
    kern = jnp.dot(features, environments.T, preferred_element_type=jnp.float32)
    kern = (kern * kern).astype(jnp.bfloat16)
    mask = (jnp.arange(BLK)[None, :] < counts[:, None]).astype(jnp.float32).reshape(ROWS, 1)
    psi = (jnp.dot(kern, projector, preferred_element_type=jnp.float32) * mask).astype(jnp.bfloat16)
    blocks = psi.reshape(NBLK, BLK, ENVS)

    def one_block(pair):
        weights, index = pair
        picked = blocks[index.astype(jnp.int32)]
        return jnp.einsum('jrc,jcm->rm', weights.astype(jnp.float32), picked.astype(jnp.float32))
    spsi = lax.map(one_block, (metric, neighbours)).reshape(ROWS, ENVS).astype(jnp.bfloat16)
    factor = 1.0 / jnp.sqrt(jnp.float32(ROWS))
    gram = jnp.dot(spsi.T, psi, preferred_element_type=jnp.float32) * factor
    rhs = jnp.dot(target, spsi.astype(jnp.float32), precision=lax.Precision.HIGHEST) * factor
    return (gram, rhs)
```

```python
import jax
import jax.numpy as jnp
from jax import lax
from jax.experimental import pallas as pl
from jax.experimental.pallas import tpu as pltpu
from jax.sharding import Mesh, PartitionSpec as P

BLK = 32
ROWS_AXES = ("y", "x", "core")
VMEM = pl.BlockSpec(memory_space=pltpu.VMEM)
SMEM = pl.BlockSpec(memory_space=pltpu.SMEM)
PARAMS = pltpu.CompilerParams(vmem_limit_bytes=48 * 1024 * 1024)


def dot(a, b, dims):
    return lax.dot_general(a, b, (dims, ((), ())), preferred_element_type=jnp.float32)


def project_kernel(counts, features, environments, projector, out):
    kern = dot(features[...], environments[...], ((1,), (1,)))
    kern = (kern * kern).astype(jnp.bfloat16)
    rows, width = kern.shape
    slots = lax.broadcasted_iota(jnp.int32, (BLK, width), 0)
    masked = jnp.concatenate(
        [
            jnp.where(slots < counts[b], kern[b * BLK:(b + 1) * BLK], jnp.bfloat16(0))
            for b in range(rows // BLK)
        ],
        axis=0,
    )
    for part in range(out.shape[0]):
        cols = slice(part * width, (part + 1) * width)
        out[part] = dot(masked, projector[:, cols], ((1,), (0,))).astype(jnp.bfloat16)


def sum_kernel(parts, out):
    total = parts[0].astype(jnp.float32)
    for part in range(1, parts.shape[0]):
        total = total + parts[part].astype(jnp.float32)
    out[...] = total.astype(jnp.bfloat16)


def metric_kernel(neighbours, before, own, after, metric, target, out, rhs, cells):
    rows = own.shape[0]
    cells[0:rows] = before[...]
    cells[rows:2 * rows] = own[...]
    cells[2 * rows:3 * rows] = after[...]
    first = neighbours[0, 0] - rows // BLK
    total = jnp.zeros((1, own.shape[1]), jnp.float32)
    for b in range(rows // BLK):
        picked = jnp.concatenate(
            [
                cells[pl.ds(pl.multiple_of((neighbours[b, j] - first) * BLK, BLK), BLK), :]
                for j in range(neighbours.shape[1])
            ],
            axis=0,
        )
        here = slice(b * BLK, (b + 1) * BLK)
        weighted = dot(metric[here, :], picked, ((1,), (0,))).astype(jnp.bfloat16)
        for copy in range(out.shape[0]):
            out[copy, here, :] = weighted
        total = total + jnp.sum(weighted.astype(jnp.float32) * target[here, :], axis=0, keepdims=True)
    rhs[...] = total


def gram_kernel(neighbours, weighted, psi, kept, sent, block):
    core = (neighbours[0, 0] // (psi.shape[0] // BLK)) % 2
    for part in range(weighted.shape[0]):
        block[...] = dot(weighted[part], psi[...], ((0,), (0,)))
        for x in range(kept.shape[1]):
            kept[part, x] = block[pl.ds(pl.multiple_of((2 * x + core) * BLK, BLK), BLK), :]
            sent[part, x] = block[
                pl.ds(pl.multiple_of((2 * x + 1 - core) * BLK, BLK), BLK), :
            ].astype(jnp.bfloat16)


def add_kernel(kept, received, out):
    for part in range(kept.shape[0]):
        out[part] = (kept[part] + received[part].astype(jnp.float32)).astype(jnp.bfloat16)


def final_kernel(parts, rhs_parts, gram, rhs, *, factor):
    total = parts[0].astype(jnp.float32)
    for part in range(1, parts.shape[0]):
        total = total + parts[part].astype(jnp.float32)
    gram[...] = total * factor
    rhs[...] = jnp.sum(rhs_parts[...], axis=0, keepdims=True) * factor


def per_device(features, environments, projector, metric, neighbours, counts, target):
    f32, bf16 = jnp.float32, jnp.bfloat16
    slab, width = features.shape[0], environments.shape[0]
    planes = lax.axis_size("env")
    ys, xs = lax.axis_size("y"), lax.axis_size("x")
    devices = ys * xs * lax.axis_size("core")
    shape = jax.ShapeDtypeStruct

    metric_rows = metric.transpose(0, 2, 1, 3).reshape(slab, -1)
    target_column = target.reshape(slab, 1)

    partial = pl.pallas_call(
        project_kernel,
        out_shape=shape((planes, slab, width), bf16),
        in_specs=[SMEM, VMEM, VMEM, VMEM],
        out_specs=VMEM,
        compiler_params=PARAMS,
    )(counts, features, environments, projector)
    partial = lax.all_to_all(partial, "env", 0, 0, tiled=True)
    psi = pl.pallas_call(
        sum_kernel,
        out_shape=shape((slab, width), bf16),
        in_specs=[VMEM],
        out_specs=VMEM,
        compiler_params=PARAMS,
    )(partial)

    before = lax.ppermute(psi, ROWS_AXES, [(i, i + 1) for i in range(devices - 1)])
    after = lax.ppermute(psi, ROWS_AXES, [(i + 1, i) for i in range(devices - 1)])
    weighted, partial_rhs = pl.pallas_call(
        metric_kernel,
        out_shape=(shape((planes, slab, width), bf16), shape((1, width), f32)),
        in_specs=[SMEM, VMEM, VMEM, VMEM, VMEM, VMEM],
        out_specs=(VMEM, VMEM),
        scratch_shapes=[pltpu.VMEM((3 * slab, width), bf16)],
        compiler_params=PARAMS,
    )(neighbours, before, psi, after, metric_rows, target_column)
    every_rhs = lax.all_gather(partial_rhs, ROWS_AXES, axis=0, tiled=True)
    weighted = lax.all_to_all(weighted, "env", 0, 0, tiled=True)

    kept, sent = pl.pallas_call(
        gram_kernel,
        out_shape=(shape((ys, xs, BLK, width), f32), shape((ys, xs, BLK, width), bf16)),
        in_specs=[SMEM, VMEM, VMEM],
        out_specs=(VMEM, VMEM),
        scratch_shapes=[pltpu.VMEM((width, width), f32)],
        compiler_params=PARAMS,
    )(neighbours, weighted, psi)
    received = lax.ppermute(sent, "core", [(0, 1), (1, 0)])
    both = pl.pallas_call(
        add_kernel,
        out_shape=shape((ys, xs, BLK, width), bf16),
        in_specs=[VMEM, VMEM],
        out_specs=VMEM,
        compiler_params=PARAMS,
    )(kept, received)
    parts = lax.all_to_all(both.reshape(ys * xs, BLK, width), ("y", "x"), 0, 0, tiled=True)

    def finish(parts, rhs_parts, gram, rhs):
        final_kernel(parts, rhs_parts, gram, rhs, factor=1.0 / (slab * devices) ** 0.5)

    gram, rhs = pl.pallas_call(
        finish,
        out_shape=(shape((BLK, width), f32), shape((1, width), f32)),
        in_specs=[VMEM, VMEM],
        out_specs=(VMEM, VMEM),
        compiler_params=PARAMS,
    )(parts, every_rhs)
    return gram, rhs.reshape(width)


def solution(mesh):
    ys, xs, cores = 8, 4, 2
    split = Mesh(mesh.devices.reshape(ys, xs, cores, mesh.shape["env"]), ("y", "x", "core", "env"))
    rows = P(ROWS_AXES)
    return jax.shard_map(
        per_device,
        mesh=split,
        in_specs=(
            P(ROWS_AXES, None),
            P("env", None),
            P("env", None),
            P(ROWS_AXES, None, None, None),
            P(ROWS_AXES, None),
            rows,
            rows,
        ),
        out_specs=(P(ROWS_AXES, "env"), P("env")),
        check_vma=False,
    )
```

```python
import jax
import jax.numpy as jnp
from jax import lax
from jax.experimental import pallas as pl
from jax.experimental.pallas import tpu as pltpu
from jax.sharding import Mesh, PartitionSpec as P

BLK = 32
EXTRA = 16
ROWS_AXES = ("y", "x", "core")
VMEM = pl.BlockSpec(memory_space=pltpu.VMEM)
SMEM = pl.BlockSpec(memory_space=pltpu.SMEM)
ANY = pl.BlockSpec(memory_space=pl.ANY)
PARAMS = pltpu.CompilerParams(vmem_limit_bytes=48 * 1024 * 1024)


def dot(a, b, dims):
    return lax.dot_general(a, b, (dims, ((), ())), preferred_element_type=jnp.float32)


def project_kernel(counts, features, environments, projector, out, slots_used, left, right, weights, sems):
    copies = [
        pltpu.make_async_copy(source, target, sems.at[i])
        for i, (source, target) in enumerate(
            [(features, left), (environments, right), (counts, slots_used), (projector, weights)]
        )
    ]
    for copy in copies:
        copy.start()
    for copy in copies[:3]:
        copy.wait()
    kern = dot(left[...], right[...], ((1,), (1,)))
    kern = (kern * kern).astype(jnp.bfloat16)
    rows, width = kern.shape
    slots = lax.broadcasted_iota(jnp.int32, (BLK, width), 0)
    masked = jnp.concatenate(
        [
            jnp.where(slots < slots_used[b], kern[b * BLK:(b + 1) * BLK], jnp.bfloat16(0))
            for b in range(rows // BLK)
        ],
        axis=0,
    )
    copies[3].wait()
    for part in range(out.shape[0]):
        cols = slice(part * width, (part + 1) * width)
        out[part] = dot(masked, weights[:, cols], ((1,), (0,))).astype(jnp.bfloat16)


def sum_kernel(parts, out):
    total = parts[0].astype(jnp.float32)
    for part in range(1, parts.shape[0]):
        total = total + parts[part].astype(jnp.float32)
    out[...] = total.astype(jnp.bfloat16)


def high_low(row, extra):
    high = row.astype(jnp.bfloat16)
    low = (row - high.astype(jnp.float32)).astype(jnp.bfloat16)
    line = lax.broadcasted_iota(jnp.int32, (extra, row.shape[1]), 0)
    return jnp.where(line == 0, high, jnp.where(line == 1, low, jnp.bfloat16(0)))


def metric_kernel(neighbours, before, own, after, metric, target, out, carried, cells):
    rows, width = own.shape
    cells[0:rows] = before[...]
    cells[rows:2 * rows] = own[...]
    cells[2 * rows:3 * rows] = after[...]
    first = neighbours[0, 0] - rows // BLK
    total = jnp.zeros((1, width), jnp.float32)
    blocks = []
    for b in range(rows // BLK):
        picked = jnp.concatenate(
            [
                cells[pl.ds(pl.multiple_of((neighbours[b, j] - first) * BLK, BLK), BLK), :]
                for j in range(neighbours.shape[1])
            ],
            axis=0,
        )
        here = slice(b * BLK, (b + 1) * BLK)
        weighted = dot(metric[here, :], picked, ((1,), (0,))).astype(jnp.bfloat16)
        blocks.append(weighted)
        total = total + jnp.sum(weighted.astype(jnp.float32) * target[here, :], axis=0, keepdims=True)
    weighted = jnp.concatenate(blocks, axis=0)
    unit = (
        lax.broadcasted_iota(jnp.int32, (rows, rows), 0) == lax.broadcasted_iota(jnp.int32, (rows, rows), 1)
    ).astype(jnp.bfloat16)
    turned = dot(weighted, unit, ((0,), (0,))).astype(jnp.bfloat16)
    group = width // BLK
    planes = out.shape[0] // group
    for j in range(group):
        for z in range(planes):
            out[j * planes + z] = turned[j * BLK:(j + 1) * BLK, :]
    carried[0:rows] = own[...]
    carried[rows:] = high_low(total, carried.shape[0] - rows)


def gram_kernel(weighted, carried, out):
    group = carried.shape[0]
    planes = weighted.shape[0] // group
    rows, width = weighted.shape[2], carried.shape[2]
    total = jnp.zeros((planes * BLK, width), jnp.float32)
    rhs = jnp.zeros((1, width), jnp.float32)
    for j in range(group):
        turned = weighted[j * planes:(j + 1) * planes].reshape(planes * BLK, rows)
        total = total + dot(turned, carried[j, 0:rows], ((1,), (0,)))
        tail = carried[j, rows:].astype(jnp.float32)
        rhs = rhs + (tail[0:1] + tail[1:2])
    extra = out.shape[1] - BLK
    lines = high_low(rhs, extra)
    for z in range(planes):
        out[z, 0:BLK] = total[z * BLK:(z + 1) * BLK].astype(jnp.bfloat16)
        out[z, BLK:] = lines


def final_kernel(parts, gram, rhs, *, factor):
    total = parts[0].astype(jnp.float32)
    for part in range(1, parts.shape[0]):
        total = total + parts[part].astype(jnp.float32)
    gram[...] = total[0:BLK] * factor
    rhs[...] = (total[BLK:BLK + 1] + total[BLK + 1:BLK + 2]) * factor


def per_device(features, environments, projector, metric, neighbours, counts, target):
    f32, bf16 = jnp.float32, jnp.bfloat16
    slab, width = features.shape[0], environments.shape[0]
    planes, ys = lax.axis_size("env"), lax.axis_size("y")
    group = lax.axis_size("x") * lax.axis_size("core")
    devices = ys * group
    shape = jax.ShapeDtypeStruct

    metric_rows = metric.transpose(0, 2, 1, 3).reshape(slab, -1)
    target_column = target.reshape(slab, 1)

    partial = pl.pallas_call(
        project_kernel,
        out_shape=shape((planes, slab, width), bf16),
        in_specs=[ANY] * 4,
        out_specs=VMEM,
        scratch_shapes=[
            pltpu.SMEM(counts.shape, jnp.int32),
            pltpu.VMEM(features.shape, bf16),
            pltpu.VMEM(environments.shape, bf16),
            pltpu.VMEM(projector.shape, bf16),
            pltpu.SemaphoreType.DMA((4,)),
        ],
        compiler_params=PARAMS,
    )(counts, features, environments, projector)
    partial = lax.all_to_all(partial, "env", 0, 0, tiled=True)
    psi = pl.pallas_call(
        sum_kernel,
        out_shape=shape((slab, width), bf16),
        in_specs=[VMEM],
        out_specs=VMEM,
        compiler_params=PARAMS,
    )(partial)

    before = lax.ppermute(psi, ROWS_AXES, [(i, i + 1) for i in range(devices - 1)])
    after = lax.ppermute(psi, ROWS_AXES, [(i + 1, i) for i in range(devices - 1)])
    weighted, carried = pl.pallas_call(
        metric_kernel,
        out_shape=(shape((group * planes, BLK, slab), bf16), shape((slab + EXTRA, width), bf16)),
        in_specs=[SMEM, VMEM, VMEM, VMEM, VMEM, VMEM],
        out_specs=(VMEM, VMEM),
        scratch_shapes=[pltpu.VMEM((3 * slab, width), bf16)],
        compiler_params=PARAMS,
    )(neighbours, before, psi, after, metric_rows, target_column)
    carried = lax.all_gather(carried, ("x", "core"), axis=0)
    weighted = lax.all_to_all(weighted, ("x", "core", "env"), 0, 0, tiled=True)
    terms = pl.pallas_call(
        gram_kernel,
        out_shape=shape((ys, BLK + EXTRA, width), bf16),
        in_specs=[VMEM, VMEM],
        out_specs=VMEM,
        compiler_params=PARAMS,
    )(weighted, carried)
    terms = lax.all_to_all(terms, "y", 0, 0, tiled=True)

    def finish(parts, gram, rhs):
        final_kernel(parts, gram, rhs, factor=1.0 / (slab * devices) ** 0.5)

    gram, rhs = pl.pallas_call(
        finish,
        out_shape=(shape((BLK, width), f32), shape((1, width), f32)),
        in_specs=[VMEM],
        out_specs=(VMEM, VMEM),
        compiler_params=PARAMS,
    )(terms)
    return gram, rhs.reshape(width)


def solution(mesh):
    ys, xs, cores = 8, 4, 2
    split = Mesh(mesh.devices.reshape(ys, xs, cores, mesh.shape["env"]), ("y", "x", "core", "env"))
    rows = P(ROWS_AXES)
    return jax.shard_map(
        per_device,
        mesh=split,
        in_specs=(
            P(ROWS_AXES, None),
            P("env", None),
            P("env", None),
            P(ROWS_AXES, None, None, None),
            P(ROWS_AXES, None),
            rows,
            rows,
        ),
        out_specs=(P(ROWS_AXES, "env"), P("env")),
        check_vma=False,
    )
```

```python
import jax
import jax.numpy as jnp
from jax import lax
from jax.experimental import pallas as pl
from jax.experimental.pallas import tpu as pltpu
from jax.sharding import Mesh, PartitionSpec as P

BLK = 32
EXTRA = 16
ROWS_AXES = ("y", "x", "core")
VMEM = pl.BlockSpec(memory_space=pltpu.VMEM)
SMEM = pl.BlockSpec(memory_space=pltpu.SMEM)
ANY = pl.BlockSpec(memory_space=pl.ANY)
PARAMS = pltpu.CompilerParams(vmem_limit_bytes=40 * 1024 * 1024)
WHOLE = pltpu.CompilerParams(vmem_limit_bytes=60 * 1024 * 1024)


def dot(a, b, dims):
    return lax.dot_general(a, b, (dims, ((), ())), preferred_element_type=jnp.float32)


def project_kernel(counts, features, environments, projector, out, slots_used, left, right, weights, sems):
    copies = [
        pltpu.make_async_copy(source, target, sems.at[i])
        for i, (source, target) in enumerate(
            [(features, left), (environments, right), (counts, slots_used), (projector, weights)]
        )
    ]
    for copy in copies:
        copy.start()
    for copy in copies[:3]:
        copy.wait()
    kern = dot(left[...], right[...], ((1,), (1,)))
    kern = (kern * kern).astype(jnp.bfloat16)
    rows, width = kern.shape
    slots = lax.broadcasted_iota(jnp.int32, (BLK, width), 0)
    masked = jnp.concatenate(
        [
            jnp.where(slots < slots_used[b], kern[b * BLK:(b + 1) * BLK], jnp.bfloat16(0))
            for b in range(rows // BLK)
        ],
        axis=0,
    )
    copies[3].wait()
    for part in range(out.shape[0]):
        cols = slice(part * width, (part + 1) * width)
        out[part] = dot(masked, weights[:, cols], ((1,), (0,))).astype(jnp.bfloat16)


def sum_kernel(parts, out):
    total = parts[0].astype(jnp.float32)
    for part in range(1, parts.shape[0]):
        total = total + parts[part].astype(jnp.float32)
    out[...] = total.astype(jnp.bfloat16)


def high_low(row, extra):
    high = row.astype(jnp.bfloat16)
    low = (row - high.astype(jnp.float32)).astype(jnp.bfloat16)
    line = lax.broadcasted_iota(jnp.int32, (extra, row.shape[1]), 0)
    return jnp.where(line == 0, high, jnp.where(line == 1, low, jnp.bfloat16(0)))


def metric_kernel(neighbours, before, own, after, metric, target, out, carried, cells):
    rows, width = own.shape
    cells[0:rows] = before[...]
    cells[rows:2 * rows] = own[...]
    cells[2 * rows:3 * rows] = after[...]
    first = neighbours[0, 0] - rows // BLK
    total = jnp.zeros((1, width), jnp.float32)
    blocks = []
    for b in range(rows // BLK):
        picked = jnp.concatenate(
            [
                cells[pl.ds(pl.multiple_of((neighbours[b, j] - first) * BLK, BLK), BLK), :]
                for j in range(neighbours.shape[1])
            ],
            axis=0,
        )
        here = slice(b * BLK, (b + 1) * BLK)
        weighted = dot(metric[here, :], picked, ((1,), (0,))).astype(jnp.bfloat16)
        blocks.append(weighted)
        total = total + jnp.sum(weighted.astype(jnp.float32) * target[here, :], axis=0, keepdims=True)
    weighted = jnp.concatenate(blocks, axis=0)
    unit = (
        lax.broadcasted_iota(jnp.int32, (rows, rows), 0) == lax.broadcasted_iota(jnp.int32, (rows, rows), 1)
    ).astype(jnp.bfloat16)
    turned = dot(weighted, unit, ((0,), (0,))).astype(jnp.bfloat16)
    pieces, chunk = out.shape[0], out.shape[1]
    group = width // chunk
    planes = pieces // group
    for part in range(group):
        for z in range(planes):
            out[part * planes + z] = turned[part * chunk:(part + 1) * chunk, :]
    carried[0:rows] = own[...]
    carried[rows:] = high_low(total, carried.shape[0] - rows)


def gram_kernel(neighbours, weighted, own, *rest):
    carried, out = (own,) + rest[:-1], rest[-1]
    group = len(carried)
    planes = weighted.shape[0] // group
    chunk, rows, width = weighted.shape[1], weighted.shape[2], own.shape[1]
    x = neighbours[0, 0] // (2 * (rows // BLK)) % group
    total = jnp.zeros((planes * chunk, width), jnp.float32)
    rhs = jnp.zeros((1, width), jnp.float32)
    for step, cells in enumerate(carried):
        source = (x + group - step) % group
        turned = weighted[pl.ds(source * planes, planes)].reshape(planes * chunk, rows)
        total = total + dot(turned, cells[0:rows], ((1,), (0,)))
        tail = cells[rows:].astype(jnp.float32)
        rhs = rhs + (tail[0:1] + tail[1:2])
    lines = high_low(rhs, EXTRA)
    half = width // 2
    lines = jnp.where(
        lax.broadcasted_iota(jnp.int32, (EXTRA, half), 0) < 2,
        lines[:, :half],
        jnp.concatenate([lines[EXTRA - 2:, half:], lines[:EXTRA - 2, half:]], axis=0),
    )
    for part in range(out.shape[0]):
        here = total[part * BLK:(part + 1) * BLK].astype(jnp.bfloat16)
        out[part, 0:BLK] = here[:, :half]
        out[part, BLK:2 * BLK] = here[:, half:]
        out[part, 2 * BLK:] = lines


def final_kernel(parts, gram, rhs, *, factor):
    total = parts[0].astype(jnp.float32)
    for part in range(1, parts.shape[0]):
        total = total + parts[part].astype(jnp.float32)
    half = total.shape[1]
    gram[:, :half] = total[0:BLK] * factor
    gram[:, half:] = total[BLK:2 * BLK] * factor
    tail = 2 * BLK
    rhs[:, :half] = (total[tail:tail + 1] + total[tail + 1:tail + 2]) * factor
    rhs[:, half:] = (total[tail + 2:tail + 3] + total[tail + 3:tail + 4]) * factor


def per_device(features, environments, projector, metric, neighbours, counts, target):
    f32, bf16 = jnp.float32, jnp.bfloat16
    slab, width = features.shape[0], environments.shape[0]
    planes, ys = lax.axis_size("env"), lax.axis_size("y")
    group, cores = lax.axis_size("x"), lax.axis_size("core")
    devices = ys * group * cores
    shape = jax.ShapeDtypeStruct

    metric_rows = metric.transpose(0, 2, 1, 3).reshape(slab, -1)
    target_column = target.reshape(slab, 1)

    partial = pl.pallas_call(
        project_kernel,
        out_shape=shape((planes, slab, width), bf16),
        in_specs=[ANY] * 4,
        out_specs=VMEM,
        scratch_shapes=[
            pltpu.SMEM(counts.shape, jnp.int32),
            pltpu.VMEM(features.shape, bf16),
            pltpu.VMEM(environments.shape, bf16),
            pltpu.VMEM(projector.shape, bf16),
            pltpu.SemaphoreType.DMA((4,)),
        ],
        compiler_params=WHOLE,
    )(counts, features, environments, projector)
    partial = lax.all_to_all(partial, "env", 0, 0, tiled=True)
    psi = pl.pallas_call(
        sum_kernel,
        out_shape=shape((slab, width), bf16),
        in_specs=[VMEM],
        out_specs=VMEM,
        compiler_params=PARAMS,
    )(partial)

    before = lax.ppermute(psi, ROWS_AXES, [(i, i + 1) for i in range(devices - 1)])
    after = lax.ppermute(psi, ROWS_AXES, [(i + 1, i) for i in range(devices - 1)])
    weighted, carried = pl.pallas_call(
        metric_kernel,
        out_shape=(shape((group * planes, width // group, slab), bf16), shape((slab + EXTRA, width), bf16)),
        in_specs=[SMEM, VMEM, VMEM, VMEM, VMEM, VMEM],
        out_specs=(VMEM, VMEM),
        scratch_shapes=[pltpu.VMEM((3 * slab, width), bf16)],
        compiler_params=PARAMS,
    )(neighbours, before, psi, after, metric_rows, target_column)
    shifted = [
        lax.ppermute(carried, "x", [(i, (i + step) % group) for i in range(group)])
        for step in range(1, group)
    ]
    weighted = lax.all_to_all(weighted, ("x", "env"), 0, 0, tiled=True)
    terms = pl.pallas_call(
        gram_kernel,
        out_shape=shape((ys * cores, 2 * BLK + EXTRA, width // 2), bf16),
        in_specs=[SMEM] + [VMEM] * (1 + group),
        out_specs=VMEM,
        compiler_params=PARAMS,
    )(neighbours, weighted, carried, *shifted)
    terms = lax.all_to_all(terms, ("y", "core"), 0, 0, tiled=True)

    def finish(parts, gram, rhs):
        final_kernel(parts, gram, rhs, factor=1.0 / (slab * devices) ** 0.5)

    gram, rhs = pl.pallas_call(
        finish,
        out_shape=(shape((BLK, width), f32), shape((1, width), f32)),
        in_specs=[VMEM],
        out_specs=(VMEM, VMEM),
        compiler_params=PARAMS,
    )(terms)
    return gram, rhs.reshape(width)


def solution(mesh):
    ys, xs, cores = 8, 4, 2
    split = Mesh(mesh.devices.reshape(ys, xs, cores, mesh.shape["env"]), ("y", "x", "core", "env"))
    rows = P(ROWS_AXES)
    return jax.shard_map(
        per_device,
        mesh=split,
        in_specs=(
            P(ROWS_AXES, None),
            P("env", None),
            P("env", None),
            P(ROWS_AXES, None, None, None),
            P(ROWS_AXES, None),
            rows,
            rows,
        ),
        out_specs=(P(ROWS_AXES, "env"), P("env")),
        check_vma=False,
    )
```

```python
import jax
import jax.numpy as jnp
from jax import lax
from jax.experimental import pallas as pl
from jax.experimental.pallas import tpu as pltpu
from jax.sharding import Mesh, PartitionSpec as P

BLK = 32
EXTRA = 16
LANES = 128
ROWS_AXES = ("y", "x", "core")
VMEM = pl.BlockSpec(memory_space=pltpu.VMEM)
SMEM = pl.BlockSpec(memory_space=pltpu.SMEM)
ANY = pl.BlockSpec(memory_space=pl.ANY)
PARAMS = pltpu.CompilerParams(vmem_limit_bytes=40 * 1024 * 1024)
WHOLE = pltpu.CompilerParams(vmem_limit_bytes=60 * 1024 * 1024)


def dot(a, b, dims):
    return lax.dot_general(a, b, (dims, ((), ())), preferred_element_type=jnp.float32)


def project_kernel(counts, features, environments, projector, out, slots_used, left, right, weights, sems):
    copies = [
        pltpu.make_async_copy(source, target, sems.at[i])
        for i, (source, target) in enumerate(
            [(features, left), (environments, right), (counts, slots_used), (projector, weights)]
        )
    ]
    for copy in copies:
        copy.start()
    for copy in copies[:3]:
        copy.wait()
    kern = dot(left[...], right[...], ((1,), (1,)))
    kern = (kern * kern).astype(jnp.bfloat16)
    rows, width = kern.shape
    slots = lax.broadcasted_iota(jnp.int32, (BLK, width), 0)
    masked = jnp.concatenate(
        [
            jnp.where(slots < slots_used[b], kern[b * BLK:(b + 1) * BLK], jnp.bfloat16(0))
            for b in range(rows // BLK)
        ],
        axis=0,
    )
    copies[3].wait()
    for part in range(out.shape[0]):
        cols = slice(part * width, (part + 1) * width)
        out[part] = dot(masked, weights[:, cols], ((1,), (0,))).astype(jnp.bfloat16)


def sum_kernel(parts, psi, out):
    total = parts[0].astype(jnp.float32)
    for part in range(1, parts.shape[0]):
        total = total + parts[part].astype(jnp.float32)
    total = total.astype(jnp.bfloat16)
    psi[...] = total
    rows, width = total.shape
    unit = (
        lax.broadcasted_iota(jnp.int32, (rows, rows), 0) == lax.broadcasted_iota(jnp.int32, (rows, rows), 1)
    ).astype(jnp.bfloat16)
    turned = dot(total, unit, ((0,), (0,))).astype(jnp.bfloat16)
    pieces, chunk = out.shape[0], out.shape[1]
    group = width // chunk
    planes = pieces // group
    for part in range(group):
        for z in range(planes):
            out[part * planes + z] = turned[part * chunk:(part + 1) * chunk, :]


def high_low(row, extra):
    high = row.astype(jnp.bfloat16)
    low = (row - high.astype(jnp.float32)).astype(jnp.bfloat16)
    line = lax.broadcasted_iota(jnp.int32, (extra, row.shape[1]), 0)
    return jnp.where(line == 0, high, jnp.where(line == 1, low, jnp.bfloat16(0)))


def spread_kernel(neighbours, psi, metric, target, before, own, after, cells):
    rows, width = psi.shape
    cells[...] = jnp.zeros_like(cells)
    first = neighbours[0, 0] - rows // BLK
    high = target[...].astype(jnp.bfloat16)
    low = (target[...] - high.astype(jnp.float32)).astype(jnp.bfloat16)
    lane = lax.broadcasted_iota(jnp.int32, (rows, LANES), 1)
    column = jnp.where(lane == 0, high, jnp.where(lane == 1, low, jnp.bfloat16(0)))
    wide = jnp.concatenate([psi[...], column], axis=1)
    for b in range(rows // BLK):
        here = slice(b * BLK, (b + 1) * BLK)
        terms = dot(metric[here, :], wide[here, :], ((0,), (0,)))
        for j in range(neighbours.shape[1]):
            there = pl.ds(pl.multiple_of((neighbours[b, j] - first) * BLK, BLK), BLK)
            cells[there, :] = cells[there, :] + terms[j * BLK:(j + 1) * BLK]
    lane = lax.broadcasted_iota(jnp.int32, (rows, LANES), 1)
    for out, start in ((before, 0), (after, 2 * rows)):
        block = cells[start:start + rows]
        weight = block[:, width:width + 1] + block[:, width + 1:width + 2]
        high = weight.astype(jnp.bfloat16)
        low = (weight - high.astype(jnp.float32)).astype(jnp.bfloat16)
        out[:, :width] = block[:, :width].astype(jnp.bfloat16)
        out[:, width:] = jnp.where(lane == 0, high, jnp.where(lane == 1, low, jnp.bfloat16(0)))
    own[...] = cells[rows:2 * rows]


def weighted_kernel(psi, own, left, right, carried):
    rows, width = psi.shape
    total = own[...] + left[...].astype(jnp.float32) + right[...].astype(jnp.float32)
    carried[0:rows] = total[:, :width].astype(jnp.bfloat16)
    weight = total[:, width:width + 1] + total[:, width + 1:width + 2]
    rhs = jnp.sum(psi[...].astype(jnp.float32) * weight, axis=0, keepdims=True)
    carried[rows:] = high_low(rhs, carried.shape[0] - rows)


def gram_kernel(neighbours, pieces, own, *rest):
    carried, out = (own,) + rest[:-1], rest[-1]
    group = len(carried)
    planes = pieces.shape[0] // group
    chunk, rows, width = pieces.shape[1], pieces.shape[2], own.shape[1]
    x = neighbours[0, 0] // (2 * (rows // BLK)) % group
    total = jnp.zeros((planes * chunk, width), jnp.float32)
    rhs = jnp.zeros((1, width), jnp.float32)
    for step, cells in enumerate(carried):
        source = (x + group - step) % group
        turned = pieces[pl.ds(source * planes, planes)].reshape(planes * chunk, rows)
        total = total + dot(turned, cells[0:rows], ((1,), (0,)))
        tail = cells[rows:].astype(jnp.float32)
        rhs = rhs + (tail[0:1] + tail[1:2])
    lines = high_low(rhs, EXTRA)
    half = width // 2
    lines = jnp.where(
        lax.broadcasted_iota(jnp.int32, (EXTRA, half), 0) < 2,
        lines[:, :half],
        jnp.concatenate([lines[EXTRA - 2:, half:], lines[:EXTRA - 2, half:]], axis=0),
    )
    for part in range(out.shape[0]):
        here = total[part * BLK:(part + 1) * BLK].astype(jnp.bfloat16)
        out[part, 0:BLK] = here[:, :half]
        out[part, BLK:2 * BLK] = here[:, half:]
        out[part, 2 * BLK:] = lines


def final_kernel(parts, gram, rhs, *, factor):
    total = parts[0].astype(jnp.float32)
    for part in range(1, parts.shape[0]):
        total = total + parts[part].astype(jnp.float32)
    half = total.shape[1]
    gram[:, :half] = total[0:BLK] * factor
    gram[:, half:] = total[BLK:2 * BLK] * factor
    tail = 2 * BLK
    rhs[:, :half] = (total[tail:tail + 1] + total[tail + 1:tail + 2]) * factor
    rhs[:, half:] = (total[tail + 2:tail + 3] + total[tail + 3:tail + 4]) * factor


def per_device(features, environments, projector, metric, neighbours, counts, target):
    f32, bf16 = jnp.float32, jnp.bfloat16
    slab, width = features.shape[0], environments.shape[0]
    planes, ys = lax.axis_size("env"), lax.axis_size("y")
    group, cores = lax.axis_size("x"), lax.axis_size("core")
    devices = ys * group * cores
    shape = jax.ShapeDtypeStruct

    metric_rows = metric.transpose(0, 2, 1, 3).reshape(slab, -1)
    target_column = target.reshape(slab, 1)

    partial = pl.pallas_call(
        project_kernel,
        out_shape=shape((planes, slab, width), bf16),
        in_specs=[ANY] * 4,
        out_specs=VMEM,
        scratch_shapes=[
            pltpu.SMEM(counts.shape, jnp.int32),
            pltpu.VMEM(features.shape, bf16),
            pltpu.VMEM(environments.shape, bf16),
            pltpu.VMEM(projector.shape, bf16),
            pltpu.SemaphoreType.DMA((4,)),
        ],
        compiler_params=WHOLE,
    )(counts, features, environments, projector)
    partial = lax.all_to_all(partial, "env", 0, 0, tiled=True)
    psi, turned = pl.pallas_call(
        sum_kernel,
        out_shape=(shape((slab, width), bf16), shape((group * planes, width // group, slab), bf16)),
        in_specs=[VMEM],
        out_specs=(VMEM, VMEM),
        compiler_params=PARAMS,
    )(partial)
    wide = shape((slab, width + LANES), bf16)
    to_before, own, to_after = pl.pallas_call(
        spread_kernel,
        out_shape=(wide, shape(wide.shape, f32), wide),
        in_specs=[SMEM, VMEM, VMEM, VMEM],
        out_specs=(VMEM, VMEM, VMEM),
        scratch_shapes=[pltpu.VMEM((3 * slab, width + LANES), f32)],
        compiler_params=PARAMS,
    )(neighbours, psi, metric_rows, target_column)
    from_after = lax.ppermute(to_before, ROWS_AXES, [(i + 1, i) for i in range(devices - 1)])
    from_before = lax.ppermute(to_after, ROWS_AXES, [(i, i + 1) for i in range(devices - 1)])
    turned = lax.all_to_all(turned, ("x", "env"), 0, 0, tiled=True)
    carried = pl.pallas_call(
        weighted_kernel,
        out_shape=shape((slab + EXTRA, width), bf16),
        in_specs=[VMEM] * 4,
        out_specs=VMEM,
        compiler_params=PARAMS,
    )(psi, own, from_before, from_after)
    shifted = [
        lax.ppermute(carried, "x", [(i, (i + step) % group) for i in range(group)])
        for step in range(1, group)
    ]
    terms = pl.pallas_call(
        gram_kernel,
        out_shape=shape((ys * cores, 2 * BLK + EXTRA, width // 2), bf16),
        in_specs=[SMEM] + [VMEM] * (1 + group),
        out_specs=VMEM,
        compiler_params=PARAMS,
    )(neighbours, turned, carried, *shifted)
    terms = lax.all_to_all(terms, ("y", "core"), 0, 0, tiled=True)

    def finish(parts, gram, rhs):
        final_kernel(parts, gram, rhs, factor=1.0 / (slab * devices) ** 0.5)

    gram, rhs = pl.pallas_call(
        finish,
        out_shape=(shape((BLK, width), f32), shape((1, width), f32)),
        in_specs=[VMEM],
        out_specs=(VMEM, VMEM),
        compiler_params=PARAMS,
    )(terms)
    return gram, rhs.reshape(width)


def solution(mesh):
    ys, xs, cores = 8, 4, 2
    split = Mesh(mesh.devices.reshape(ys, xs, cores, mesh.shape["env"]), ("y", "x", "core", "env"))
    rows = P(ROWS_AXES)
    return jax.shard_map(
        per_device,
        mesh=split,
        in_specs=(
            P(ROWS_AXES, None),
            P("env", None),
            P("env", None),
            P(ROWS_AXES, None, None, None),
            P(ROWS_AXES, None),
            rows,
            rows,
        ),
        out_specs=(P(ROWS_AXES, "env"), P("env")),
        check_vma=False,
    )
```

```python
import jax
import jax.numpy as jnp
from jax import lax
from jax.experimental import pallas as pl
from jax.experimental.pallas import tpu as pltpu
from jax.sharding import Mesh, PartitionSpec as P

BLK = 32
EXTRA = 16
LANES = 128
ROWS_AXES = ("y", "x", "core")
VMEM = pl.BlockSpec(memory_space=pltpu.VMEM)
SMEM = pl.BlockSpec(memory_space=pltpu.SMEM)
ANY = pl.BlockSpec(memory_space=pl.ANY)
PARAMS = pltpu.CompilerParams(vmem_limit_bytes=40 * 1024 * 1024)
WHOLE = pltpu.CompilerParams(vmem_limit_bytes=60 * 1024 * 1024)


def dot(a, b, dims):
    return lax.dot_general(a, b, (dims, ((), ())), preferred_element_type=jnp.float32)


def project_kernel(
    counts, features, environments, projector, out, slots_used, left, right, weights, parts, sems, sent
):
    copies = [
        pltpu.make_async_copy(source, target, sems.at[i])
        for i, (source, target) in enumerate(
            [(features, left), (environments, right), (counts, slots_used), (projector, weights)]
        )
    ]
    for copy in copies:
        copy.start()
    for copy in copies[:3]:
        copy.wait()
    kern = dot(left[...], right[...], ((1,), (1,)))
    kern = (kern * kern).astype(jnp.bfloat16)
    rows, width = kern.shape
    slots = lax.broadcasted_iota(jnp.int32, (BLK, width), 0)
    masked = jnp.concatenate(
        [
            jnp.where(slots < slots_used[b], kern[b * BLK:(b + 1) * BLK], jnp.bfloat16(0))
            for b in range(rows // BLK)
        ],
        axis=0,
    )
    copies[3].wait()
    for part in range(out.shape[0]):
        cols = slice(part * width, (part + 1) * width)
        parts[part] = dot(masked, weights[:, cols], ((1,), (0,))).astype(jnp.bfloat16)
        pltpu.make_async_copy(parts.at[part], out.at[part], sent.at[part]).start()
    for part in range(out.shape[0]):
        pltpu.make_async_copy(parts.at[part], out.at[part], sent.at[part]).wait()


def sum_kernel(parts, metric, target, psi, out):
    del metric, target
    total = parts[0].astype(jnp.float32)
    for part in range(1, parts.shape[0]):
        total = total + parts[part].astype(jnp.float32)
    total = total.astype(jnp.bfloat16)
    psi[...] = total
    rows, width = total.shape
    unit = (
        lax.broadcasted_iota(jnp.int32, (rows, rows), 0) == lax.broadcasted_iota(jnp.int32, (rows, rows), 1)
    ).astype(jnp.bfloat16)
    turned = dot(total, unit, ((0,), (0,))).astype(jnp.bfloat16)
    pieces, chunk = out.shape[0], out.shape[1]
    group = width // chunk
    planes = pieces // group
    for part in range(group):
        for z in range(planes):
            out[part * planes + z] = turned[part * chunk:(part + 1) * chunk, :]


def high_low(row, extra):
    high = row.astype(jnp.bfloat16)
    low = (row - high.astype(jnp.float32)).astype(jnp.bfloat16)
    line = lax.broadcasted_iota(jnp.int32, (extra, row.shape[1]), 0)
    return jnp.where(line == 0, high, jnp.where(line == 1, low, jnp.bfloat16(0)))


def spread_kernel(neighbours, psi, metric, target, before, own, after, cells):
    rows, width = psi.shape
    cells[...] = jnp.zeros_like(cells)
    first = neighbours[0, 0] - rows // BLK
    high = target[...].astype(jnp.bfloat16)
    low = (target[...] - high.astype(jnp.float32)).astype(jnp.bfloat16)
    lane = lax.broadcasted_iota(jnp.int32, (rows, LANES), 1)
    column = jnp.where(lane == 0, high, jnp.where(lane == 1, low, jnp.bfloat16(0)))
    wide = jnp.concatenate([psi[...], column], axis=1)
    for b in range(rows // BLK):
        here = slice(b * BLK, (b + 1) * BLK)
        terms = dot(metric[here, :], wide[here, :], ((0,), (0,)))
        for j in range(neighbours.shape[1]):
            there = pl.ds(pl.multiple_of((neighbours[b, j] - first) * BLK, BLK), BLK)
            cells[there, :] = cells[there, :] + terms[j * BLK:(j + 1) * BLK]
    lane = lax.broadcasted_iota(jnp.int32, (rows, LANES), 1)
    for out, start in ((before, 0), (after, 2 * rows)):
        block = cells[start:start + rows]
        weight = block[:, width:width + 1] + block[:, width + 1:width + 2]
        high = weight.astype(jnp.bfloat16)
        low = (weight - high.astype(jnp.float32)).astype(jnp.bfloat16)
        out[:, :width] = block[:, :width].astype(jnp.bfloat16)
        out[:, width:] = jnp.where(lane == 0, high, jnp.where(lane == 1, low, jnp.bfloat16(0)))
    own[...] = cells[rows:2 * rows]


def weighted_kernel(psi, own, left, right, carried):
    rows, width = psi.shape
    total = own[...] + left[...].astype(jnp.float32) + right[...].astype(jnp.float32)
    carried[0:rows] = total[:, :width].astype(jnp.bfloat16)
    weight = total[:, width:width + 1] + total[:, width + 1:width + 2]
    rhs = jnp.sum(psi[...].astype(jnp.float32) * weight, axis=0, keepdims=True)
    carried[rows:] = high_low(rhs, carried.shape[0] - rows)


def gram_kernel(neighbours, pieces, own, *rest):
    carried, (kept, sent, block) = (own,) + rest[:-3], rest[-3:]
    group = len(carried)
    planes = pieces.shape[0] // group
    chunk, rows, width = pieces.shape[1], pieces.shape[2], own.shape[1]
    x = neighbours[0, 0] // (2 * (rows // BLK)) % group
    total = jnp.zeros((planes * chunk, width), jnp.float32)
    rhs = jnp.zeros((1, width), jnp.float32)
    for step, cells in enumerate(carried):
        source = (x + group - step) % group
        turned = pieces[pl.ds(source * planes, planes)].reshape(planes * chunk, rows)
        total = total + dot(turned, cells[0:rows], ((1,), (0,)))
        tail = cells[rows:].astype(jnp.float32)
        rhs = rhs + (tail[0:1] + tail[1:2])
    lines = high_low(rhs, EXTRA)
    half = width // 2
    block[...] = total
    core = neighbours[0, 0] // (rows // BLK) % 2
    row = lax.broadcasted_iota(jnp.int32, (EXTRA, half), 0)
    tail = jnp.where(row == 0, rhs[:, :half], jnp.where(row == 2, rhs[:, half:], 0.0))
    for part in range(kept.shape[0]):
        here = block[pl.ds(pl.multiple_of((2 * part + core) * BLK, BLK), BLK), :]
        kept[part, 0:BLK] = here[:, :half]
        kept[part, BLK:2 * BLK] = here[:, half:]
        kept[part, 2 * BLK:] = tail
        here = block[pl.ds(pl.multiple_of((2 * part + 1 - core) * BLK, BLK), BLK), :].astype(jnp.bfloat16)
        sent[part, 0:BLK] = here[:, :half]
        sent[part, BLK:2 * BLK] = here[:, half:]
        sent[part, 2 * BLK:] = split_rows(tail)


def split_rows(tail):
    high = tail.astype(jnp.bfloat16)
    low = (tail - high.astype(jnp.float32)).astype(jnp.bfloat16)
    low = jnp.concatenate([low[-1:], low[:-1]], axis=0)
    row = lax.broadcasted_iota(jnp.int32, tail.shape, 0)
    return jnp.where(row % 2 == 0, high, low)


def add_kernel(kept, received, out):
    total = kept[...] + received[...].astype(jnp.float32)
    tail = total[0, 2 * BLK:]
    row = lax.broadcasted_iota(jnp.int32, tail.shape, 0)
    first, second = tail[0:1] + tail[1:2], tail[2:3] + tail[3:4]
    tail = split_rows(jnp.where(row == 0, first, jnp.where(row == 2, second, 0.0)))
    for part in range(out.shape[0]):
        out[part, 0:2 * BLK] = total[part, 0:2 * BLK].astype(jnp.bfloat16)
        out[part, 2 * BLK:] = tail


def final_kernel(parts, gram, rhs, *, factor):
    total = parts[0].astype(jnp.float32)
    for part in range(1, parts.shape[0]):
        total = total + parts[part].astype(jnp.float32)
    half = total.shape[1]
    gram[:, :half] = total[0:BLK] * factor
    gram[:, half:] = total[BLK:2 * BLK] * factor
    tail = 2 * BLK
    rhs[:, :half] = (total[tail:tail + 1] + total[tail + 1:tail + 2]) * factor
    rhs[:, half:] = (total[tail + 2:tail + 3] + total[tail + 3:tail + 4]) * factor


def per_device(features, environments, projector, metric, neighbours, counts, target):
    f32, bf16 = jnp.float32, jnp.bfloat16
    slab, width = features.shape[0], environments.shape[0]
    planes, ys = lax.axis_size("env"), lax.axis_size("y")
    group, cores = lax.axis_size("x"), lax.axis_size("core")
    devices = ys * group * cores
    shape = jax.ShapeDtypeStruct

    metric_rows = metric.transpose(0, 2, 1, 3).reshape(slab, -1)
    target_column = target.reshape(slab, 1)

    partial = pl.pallas_call(
        project_kernel,
        out_shape=shape((planes, slab, width), bf16),
        in_specs=[ANY] * 4,
        out_specs=ANY,
        scratch_shapes=[
            pltpu.SMEM(counts.shape, jnp.int32),
            pltpu.VMEM(features.shape, bf16),
            pltpu.VMEM(environments.shape, bf16),
            pltpu.VMEM(projector.shape, bf16),
            pltpu.VMEM((planes, slab, width), bf16),
            pltpu.SemaphoreType.DMA((4,)),
            pltpu.SemaphoreType.DMA((planes,)),
        ],
        compiler_params=WHOLE,
    )(counts, features, environments, projector)
    partial = lax.all_to_all(partial, "env", 0, 0, tiled=True)
    psi, turned = pl.pallas_call(
        sum_kernel,
        out_shape=(shape((slab, width), bf16), shape((group * planes, width // group, slab), bf16)),
        in_specs=[VMEM] * 3,
        out_specs=(VMEM, VMEM),
        compiler_params=PARAMS,
    )(partial, metric_rows, target_column)
    wide = shape((slab, width + LANES), bf16)
    to_before, own, to_after = pl.pallas_call(
        spread_kernel,
        out_shape=(wide, shape(wide.shape, f32), wide),
        in_specs=[SMEM, VMEM, VMEM, VMEM],
        out_specs=(VMEM, VMEM, VMEM),
        scratch_shapes=[pltpu.VMEM((3 * slab, width + LANES), f32)],
        compiler_params=PARAMS,
    )(neighbours, psi, metric_rows, target_column)
    from_after = lax.ppermute(to_before, ROWS_AXES, [(i + 1, i) for i in range(devices - 1)])
    from_before = lax.ppermute(to_after, ROWS_AXES, [(i, i + 1) for i in range(devices - 1)])
    turned = lax.all_to_all(turned, ("x", "env"), 0, 0, tiled=True)
    carried = pl.pallas_call(
        weighted_kernel,
        out_shape=shape((slab + EXTRA, width), bf16),
        in_specs=[VMEM] * 4,
        out_specs=VMEM,
        compiler_params=PARAMS,
    )(psi, own, from_before, from_after)
    shifted = [
        lax.ppermute(carried, "x", [(i, (i + step) % group) for i in range(group)])
        for step in range(1, group)
    ]
    parts = (ys, 2 * BLK + EXTRA, width // 2)
    kept, sent = pl.pallas_call(
        gram_kernel,
        out_shape=(shape(parts, f32), shape(parts, bf16)),
        in_specs=[SMEM] + [VMEM] * (1 + group),
        out_specs=(VMEM, VMEM),
        scratch_shapes=[pltpu.VMEM((planes * width // group, width), f32)],
        compiler_params=PARAMS,
    )(neighbours, turned, carried, *shifted)
    received = lax.ppermute(sent, "core", [(0, 1), (1, 0)])
    terms = pl.pallas_call(
        add_kernel,
        out_shape=shape(parts, bf16),
        in_specs=[VMEM, VMEM],
        out_specs=VMEM,
        compiler_params=PARAMS,
    )(kept, received)
    terms = lax.all_to_all(terms, "y", 0, 0, tiled=True)

    def finish(parts, gram, rhs):
        final_kernel(parts, gram, rhs, factor=1.0 / (slab * devices) ** 0.5)

    gram, rhs = pl.pallas_call(
        finish,
        out_shape=(shape((BLK, width), f32), shape((1, width), f32)),
        in_specs=[VMEM],
        out_specs=(VMEM, VMEM),
        compiler_params=PARAMS,
    )(terms)
    return gram, rhs.reshape(width)


def solution(mesh):
    ys, xs, cores = 8, 4, 2
    split = Mesh(mesh.devices.reshape(ys, xs, cores, mesh.shape["env"]), ("y", "x", "core", "env"))
    rows = P(ROWS_AXES)
    return jax.shard_map(
        per_device,
        mesh=split,
        in_specs=(
            P(ROWS_AXES, None),
            P("env", None),
            P("env", None),
            P(ROWS_AXES, None, None, None),
            P(ROWS_AXES, None),
            rows,
            rows,
        ),
        out_specs=(P(ROWS_AXES, "env"), P("env")),
        check_vma=False,
    )
```

```python
import jax
import jax.numpy as jnp
from jax import lax
from jax.experimental import pallas as pl
from jax.experimental.pallas import tpu as pltpu
from jax.sharding import Mesh, PartitionSpec as P

BLK = 32
EXTRA = 16
LANES = 128
ROWS_AXES = ("y", "x", "core")
VMEM = pl.BlockSpec(memory_space=pltpu.VMEM)
SMEM = pl.BlockSpec(memory_space=pltpu.SMEM)
ANY = pl.BlockSpec(memory_space=pl.ANY)
PARAMS = pltpu.CompilerParams(vmem_limit_bytes=40 * 1024 * 1024)
WHOLE = pltpu.CompilerParams(vmem_limit_bytes=60 * 1024 * 1024)


def dot(a, b, dims):
    return lax.dot_general(a, b, (dims, ((), ())), preferred_element_type=jnp.float32)


def project_kernel(
    counts, features, environments, projector, out, slots_used, left, right, weights, parts, sems, sent
):
    copies = [
        pltpu.make_async_copy(source, target, sems.at[i])
        for i, (source, target) in enumerate(
            [(features, left), (environments, right), (counts, slots_used), (projector, weights)]
        )
    ]
    for copy in copies:
        copy.start()
    for copy in copies[:3]:
        copy.wait()
    kern = dot(left[...], right[...], ((1,), (1,)))
    kern = (kern * kern).astype(jnp.bfloat16)
    rows, width = kern.shape
    slots = lax.broadcasted_iota(jnp.int32, (BLK, width), 0)
    masked = jnp.concatenate(
        [
            jnp.where(slots < slots_used[b], kern[b * BLK:(b + 1) * BLK], jnp.bfloat16(0))
            for b in range(rows // BLK)
        ],
        axis=0,
    )
    copies[3].wait()
    for part in range(out.shape[0]):
        cols = slice(part * width, (part + 1) * width)
        parts[part] = dot(masked, weights[:, cols], ((1,), (0,))).astype(jnp.bfloat16)
        pltpu.make_async_copy(parts.at[part], out.at[part], sent.at[part]).start()
    for part in range(out.shape[0]):
        pltpu.make_async_copy(parts.at[part], out.at[part], sent.at[part]).wait()


def unit(size):
    row = lax.broadcasted_iota(jnp.int32, (size, size), 0)
    return (row == lax.broadcasted_iota(jnp.int32, (size, size), 1)).astype(jnp.bfloat16)


def sum_kernel(parts, metric, target, psi, out):
    del metric, target
    total = parts[0].astype(jnp.float32)
    for part in range(1, parts.shape[0]):
        total = total + parts[part].astype(jnp.float32)
    total = total.astype(jnp.bfloat16)
    psi[...] = total
    rows, width = total.shape
    turned = dot(total, unit(rows), ((0,), (0,))).astype(jnp.bfloat16)
    pieces, chunk = out.shape[0], out.shape[1]
    group = width // chunk
    planes = pieces // group
    for part in range(group):
        for z in range(planes):
            out[part * planes + z] = turned[part * chunk:(part + 1) * chunk, :]


def high_low(row, extra):
    high = row.astype(jnp.bfloat16)
    low = (row - high.astype(jnp.float32)).astype(jnp.bfloat16)
    line = lax.broadcasted_iota(jnp.int32, (extra, row.shape[1]), 0)
    return jnp.where(line == 0, high, jnp.where(line == 1, low, jnp.bfloat16(0)))


def spread_kernel(neighbours, psi, metric, target, inner, own, outer, cells):
    rows, width = psi.shape
    cells[...] = jnp.zeros_like(cells)
    first = neighbours[0, 0] - rows // BLK
    high = target[...].astype(jnp.bfloat16)
    low = (target[...] - high.astype(jnp.float32)).astype(jnp.bfloat16)
    lane = lax.broadcasted_iota(jnp.int32, (rows, LANES), 1)
    column = jnp.where(lane == 0, high, jnp.where(lane == 1, low, jnp.bfloat16(0)))
    wide = jnp.concatenate([psi[...], column], axis=1)
    for b in range(rows // BLK):
        here = slice(b * BLK, (b + 1) * BLK)
        terms = dot(metric[here, :], wide[here, :], ((0,), (0,)))
        for j in range(neighbours.shape[1]):
            there = pl.ds(pl.multiple_of((neighbours[b, j] - first) * BLK, BLK), BLK)
            cells[there, :] = cells[there, :] + terms[j * BLK:(j + 1) * BLK]
    core = neighbours[0, 0] // (rows // BLK) % 2
    for out, start in ((inner, 2 * rows * (1 - core)), (own, rows), (outer, 2 * rows * core)):
        block = cells[pl.ds(pl.multiple_of(start, rows), rows), :]
        weight = block[:, width:width + 1] + block[:, width + 1:width + 2]
        high = weight.astype(jnp.bfloat16)
        low = (weight - high.astype(jnp.float32)).astype(jnp.bfloat16)
        column = jnp.where(lane == 0, high, jnp.where(lane == 1, low, jnp.bfloat16(0)))
        out[0:rows] = block[:, :width].astype(out.dtype)
        out[rows:] = dot(column, unit(rows), ((0,), (0,)))[0:EXTRA].astype(out.dtype)


def weighted_kernel(psi, own, inner, outer, carried):
    rows, width = psi.shape
    total = own[0:rows] + inner[0:rows].astype(jnp.float32) + outer[0:rows].astype(jnp.float32)
    carried[0:rows] = total.astype(jnp.bfloat16)
    rhs = jnp.zeros((1, width), jnp.float32)
    for cells in (own, inner, outer):
        terms = dot(cells[rows:].astype(jnp.bfloat16), psi[...], ((1,), (0,)))
        rhs = rhs + (terms[0:1] + terms[1:2])
    carried[rows:] = high_low(rhs, carried.shape[0] - rows)


def gram_kernel(neighbours, pieces, own, *rest):
    carried, (kept, sent, block) = (own,) + rest[:-3], rest[-3:]
    group = len(carried)
    planes = pieces.shape[0] // group
    chunk, rows, width = pieces.shape[1], pieces.shape[2], own.shape[1]
    x = neighbours[0, 0] // (2 * (rows // BLK)) % group
    total = jnp.zeros((planes * chunk, width), jnp.float32)
    rhs = jnp.zeros((1, width), jnp.float32)
    for step, cells in enumerate(carried):
        source = x ^ step
        turned = pieces[pl.ds(source * planes, planes)].reshape(planes * chunk, rows)
        total = total + dot(turned, cells[0:rows], ((1,), (0,)))
        tail = cells[rows:].astype(jnp.float32)
        rhs = rhs + (tail[0:1] + tail[1:2])
    lines = high_low(rhs, EXTRA)
    half = width // 2
    block[...] = total
    core = neighbours[0, 0] // (rows // BLK) % 2
    row = lax.broadcasted_iota(jnp.int32, (EXTRA, half), 0)
    tail = jnp.where(row == 0, rhs[:, :half], jnp.where(row == 2, rhs[:, half:], 0.0))
    for part in range(kept.shape[0]):
        here = block[pl.ds(pl.multiple_of((2 * part + core) * BLK, BLK), BLK), :]
        kept[part, 0:BLK] = here[:, :half]
        kept[part, BLK:2 * BLK] = here[:, half:]
        kept[part, 2 * BLK:] = tail
        here = block[pl.ds(pl.multiple_of((2 * part + 1 - core) * BLK, BLK), BLK), :].astype(jnp.bfloat16)
        sent[part, 0:BLK] = here[:, :half]
        sent[part, BLK:2 * BLK] = here[:, half:]
        sent[part, 2 * BLK:] = split_rows(tail)


def split_rows(tail):
    high = tail.astype(jnp.bfloat16)
    low = (tail - high.astype(jnp.float32)).astype(jnp.bfloat16)
    low = jnp.concatenate([low[-1:], low[:-1]], axis=0)
    row = lax.broadcasted_iota(jnp.int32, tail.shape, 0)
    return jnp.where(row % 2 == 0, high, low)


def add_kernel(kept, received, out):
    total = kept[...] + received[...].astype(jnp.float32)
    tail = total[0, 2 * BLK:]
    row = lax.broadcasted_iota(jnp.int32, tail.shape, 0)
    first, second = tail[0:1] + tail[1:2], tail[2:3] + tail[3:4]
    tail = split_rows(jnp.where(row == 0, first, jnp.where(row == 2, second, 0.0)))
    for part in range(out.shape[0]):
        out[part, 0:2 * BLK] = total[part, 0:2 * BLK].astype(jnp.bfloat16)
        out[part, 2 * BLK:] = tail


def final_kernel(parts, gram, rhs, *, factor):
    total = parts[0].astype(jnp.float32)
    for part in range(1, parts.shape[0]):
        total = total + parts[part].astype(jnp.float32)
    half = total.shape[1]
    gram[:, :half] = total[0:BLK] * factor
    gram[:, half:] = total[BLK:2 * BLK] * factor
    tail = 2 * BLK
    rhs[:, :half] = (total[tail:tail + 1] + total[tail + 1:tail + 2]) * factor
    rhs[:, half:] = (total[tail + 2:tail + 3] + total[tail + 3:tail + 4]) * factor


def per_device(features, environments, projector, metric, neighbours, counts, target):
    f32, bf16 = jnp.float32, jnp.bfloat16
    slab, width = features.shape[0], environments.shape[0]
    planes, ys = lax.axis_size("env"), lax.axis_size("y")
    group, cores = lax.axis_size("x"), lax.axis_size("core")
    devices = ys * group * cores
    shape = jax.ShapeDtypeStruct

    metric_rows = metric.transpose(0, 2, 1, 3).reshape(slab, -1)
    target_column = target.reshape(slab, 1)

    partial = pl.pallas_call(
        project_kernel,
        out_shape=shape((planes, slab, width), bf16),
        in_specs=[ANY] * 4,
        out_specs=ANY,
        scratch_shapes=[
            pltpu.SMEM(counts.shape, jnp.int32),
            pltpu.VMEM(features.shape, bf16),
            pltpu.VMEM(environments.shape, bf16),
            pltpu.VMEM(projector.shape, bf16),
            pltpu.VMEM((planes, slab, width), bf16),
            pltpu.SemaphoreType.DMA((4,)),
            pltpu.SemaphoreType.DMA((planes,)),
        ],
        compiler_params=WHOLE,
    )(counts, features, environments, projector)
    partial = lax.all_to_all(partial, "env", 0, 0, tiled=True)
    psi, turned = pl.pallas_call(
        sum_kernel,
        out_shape=(shape((slab, width), bf16), shape((group * planes, width // group, slab), bf16)),
        in_specs=[VMEM] * 3,
        out_specs=(VMEM, VMEM),
        compiler_params=PARAMS,
    )(partial, metric_rows, target_column)
    message = shape((slab + EXTRA, width), bf16)
    inner, own, outer = pl.pallas_call(
        spread_kernel,
        out_shape=(message, shape(message.shape, f32), message),
        in_specs=[SMEM] + [VMEM] * 3,
        out_specs=(VMEM,) * 3,
        scratch_shapes=[pltpu.VMEM((3 * slab, width + LANES), f32)],
        compiler_params=PARAMS,
    )(neighbours, psi, metric_rows, target_column)
    next_chip = [(i, i + 2 * (i % 2) - 1) for i in range(1, devices - 1)]
    outer = lax.ppermute(outer, ROWS_AXES, next_chip)
    inner = lax.ppermute(inner, "core", [(0, 1), (1, 0)])
    turned = lax.all_to_all(turned, ("x", "env"), 0, 0, tiled=True)
    carried = pl.pallas_call(
        weighted_kernel,
        out_shape=shape((slab + EXTRA, width), bf16),
        in_specs=[VMEM] * 4,
        out_specs=VMEM,
        compiler_params=PARAMS,
    )(psi, own, inner, outer)
    shifted = [
        lax.ppermute(carried, "x", [(i, i ^ step) for i in range(group)]) for step in range(1, group)
    ]
    parts = (ys, 2 * BLK + EXTRA, width // 2)
    kept, sent = pl.pallas_call(
        gram_kernel,
        out_shape=(shape(parts, f32), shape(parts, bf16)),
        in_specs=[SMEM] + [VMEM] * (1 + group),
        out_specs=(VMEM, VMEM),
        scratch_shapes=[pltpu.VMEM((planes * width // group, width), f32)],
        compiler_params=PARAMS,
    )(neighbours, turned, carried, *shifted)
    received = lax.ppermute(sent, "core", [(0, 1), (1, 0)])
    terms = pl.pallas_call(
        add_kernel,
        out_shape=shape(parts, bf16),
        in_specs=[VMEM, VMEM],
        out_specs=VMEM,
        compiler_params=PARAMS,
    )(kept, received)
    terms = lax.all_to_all(terms, "y", 0, 0, tiled=True)

    def finish(parts, gram, rhs):
        final_kernel(parts, gram, rhs, factor=1.0 / (slab * devices) ** 0.5)

    gram, rhs = pl.pallas_call(
        finish,
        out_shape=(shape((BLK, width), f32), shape((1, width), f32)),
        in_specs=[VMEM],
        out_specs=(VMEM, VMEM),
        compiler_params=PARAMS,
    )(terms)
    return gram, rhs.reshape(width)


def solution(mesh):
    ys, xs, cores = 8, 4, 2
    split = Mesh(mesh.devices.reshape(ys, xs, cores, mesh.shape["env"]), ("y", "x", "core", "env"))
    rows = P(ROWS_AXES)
    return jax.shard_map(
        per_device,
        mesh=split,
        in_specs=(
            P(ROWS_AXES, None),
            P("env", None),
            P("env", None),
            P(ROWS_AXES, None, None, None),
            P(ROWS_AXES, None),
            rows,
            rows,
        ),
        out_specs=(P(ROWS_AXES, "env"), P("env")),
        check_vma=False,
    )
```

```python
import jax
import jax.numpy as jnp
from jax import lax
from jax.experimental import pallas as pl
from jax.experimental.pallas import tpu as pltpu
from jax.sharding import Mesh, PartitionSpec as P

BLK = 32
EXTRA = 16
LANES = 128
ROWS_AXES = ("y", "x", "core")
ORDER = (0, 2, 4, 6, 1, 3, 5, 7)
VMEM = pl.BlockSpec(memory_space=pltpu.VMEM)
SMEM = pl.BlockSpec(memory_space=pltpu.SMEM)
ANY = pl.BlockSpec(memory_space=pl.ANY)
PARAMS = pltpu.CompilerParams(vmem_limit_bytes=40 * 1024 * 1024)
WHOLE = pltpu.CompilerParams(vmem_limit_bytes=60 * 1024 * 1024)


def dot(a, b, dims):
    return lax.dot_general(a, b, (dims, ((), ())), preferred_element_type=jnp.float32)


def project_kernel(
    counts, features, environments, projector, out, slots_used, left, right, weights, parts, sems, sent
):
    copies = [
        pltpu.make_async_copy(source, target, sems.at[i])
        for i, (source, target) in enumerate(
            [(features, left), (environments, right), (counts, slots_used), (projector, weights)]
        )
    ]
    for copy in copies:
        copy.start()
    for copy in copies[:3]:
        copy.wait()
    kern = dot(left[...], right[...], ((1,), (1,)))
    kern = (kern * kern).astype(jnp.bfloat16)
    rows, width = kern.shape
    slots = lax.broadcasted_iota(jnp.int32, (BLK, width), 0)
    masked = jnp.concatenate(
        [
            jnp.where(slots < slots_used[b], kern[b * BLK:(b + 1) * BLK], jnp.bfloat16(0))
            for b in range(rows // BLK)
        ],
        axis=0,
    )
    copies[3].wait()
    for part in range(out.shape[0]):
        cols = slice(part * width, (part + 1) * width)
        parts[part] = dot(masked, weights[:, cols], ((1,), (0,))).astype(jnp.bfloat16)
        pltpu.make_async_copy(parts.at[part], out.at[ORDER.index(part)], sent.at[part]).start()
    for part in range(out.shape[0]):
        pltpu.make_async_copy(parts.at[part], out.at[ORDER.index(part)], sent.at[part]).wait()


def unit(size):
    row = lax.broadcasted_iota(jnp.int32, (size, size), 0)
    return (row == lax.broadcasted_iota(jnp.int32, (size, size), 1)).astype(jnp.bfloat16)


def sum_kernel(parts, metric, target, psi, out):
    del metric, target
    total = parts[0].astype(jnp.float32)
    for part in range(1, parts.shape[0]):
        total = total + parts[part].astype(jnp.float32)
    total = total.astype(jnp.bfloat16)
    psi[...] = total
    rows, width = total.shape
    turned = dot(total, unit(rows), ((0,), (0,))).astype(jnp.bfloat16)
    pieces, chunk = out.shape[0], out.shape[1]
    group = width // chunk
    planes = pieces // group
    for part in range(group):
        for z in range(planes):
            out[part * planes + z] = turned[part * chunk:(part + 1) * chunk, :]


def high_low(row, extra):
    high = row.astype(jnp.bfloat16)
    low = (row - high.astype(jnp.float32)).astype(jnp.bfloat16)
    line = lax.broadcasted_iota(jnp.int32, (extra, row.shape[1]), 0)
    return jnp.where(line == 0, high, jnp.where(line == 1, low, jnp.bfloat16(0)))


def spread_kernel(neighbours, psi, metric, target, inner, own, outer, cells):
    rows, width = psi.shape
    cells[...] = jnp.zeros_like(cells)
    first = neighbours[0, 0] - rows // BLK
    high = target[...].astype(jnp.bfloat16)
    low = (target[...] - high.astype(jnp.float32)).astype(jnp.bfloat16)
    lane = lax.broadcasted_iota(jnp.int32, (rows, LANES), 1)
    column = jnp.where(lane == 0, high, jnp.where(lane == 1, low, jnp.bfloat16(0)))
    wide = jnp.concatenate([psi[...], column], axis=1)
    for b in range(rows // BLK):
        here = slice(b * BLK, (b + 1) * BLK)
        terms = dot(metric[here, :], wide[here, :], ((0,), (0,)))
        for j in range(neighbours.shape[1]):
            there = pl.ds(pl.multiple_of((neighbours[b, j] - first) * BLK, BLK), BLK)
            cells[there, :] = cells[there, :] + terms[j * BLK:(j + 1) * BLK]
    core = neighbours[0, 0] // (rows // BLK) % 2
    for out, start in ((inner, 2 * rows * (1 - core)), (own, rows), (outer, 2 * rows * core)):
        block = cells[pl.ds(pl.multiple_of(start, rows), rows), :]
        weight = block[:, width:width + 1] + block[:, width + 1:width + 2]
        high = weight.astype(jnp.bfloat16)
        low = (weight - high.astype(jnp.float32)).astype(jnp.bfloat16)
        column = jnp.where(lane == 0, high, jnp.where(lane == 1, low, jnp.bfloat16(0)))
        out[0:rows] = block[:, :width].astype(out.dtype)
        out[rows:] = dot(column, unit(rows), ((0,), (0,)))[0:EXTRA].astype(out.dtype)


def weighted_kernel(psi, own, inner, outer, carried):
    rows, width = psi.shape
    total = own[0:rows] + inner[0:rows].astype(jnp.float32) + outer[0:rows].astype(jnp.float32)
    carried[0:rows] = total.astype(jnp.bfloat16)
    rhs = jnp.zeros((1, width), jnp.float32)
    for cells in (own, inner, outer):
        terms = dot(cells[rows:].astype(jnp.bfloat16), psi[...], ((1,), (0,)))
        rhs = rhs + (terms[0:1] + terms[1:2])
    carried[rows:] = high_low(rhs, carried.shape[0] - rows)


def gram_kernel(neighbours, pieces, own, *rest):
    carried, (kept, sent, block) = (own,) + rest[:-3], rest[-3:]
    group = len(carried)
    planes = pieces.shape[0] // group
    chunk, rows, width = pieces.shape[1], pieces.shape[2], own.shape[1]
    x = neighbours[0, 0] // (2 * (rows // BLK)) % group
    total = jnp.zeros((planes * chunk, width), jnp.float32)
    rhs = jnp.zeros((1, width), jnp.float32)
    for step, cells in enumerate(carried):
        source = x ^ step
        turned = pieces[pl.ds(source * planes, planes)].reshape(planes * chunk, rows)
        total = total + dot(turned, cells[0:rows], ((1,), (0,)))
        tail = cells[rows:].astype(jnp.float32)
        rhs = rhs + (tail[0:1] + tail[1:2])
    lines = high_low(rhs, EXTRA)
    half = width // 2
    block[...] = total
    core = neighbours[0, 0] // (rows // BLK) % 2
    row = lax.broadcasted_iota(jnp.int32, (EXTRA, half), 0)
    tail = jnp.where(row == 0, rhs[:, :half], jnp.where(row == 2, rhs[:, half:], 0.0))
    for part in range(kept.shape[0]):
        here = block[pl.ds(pl.multiple_of((2 * part + core) * BLK, BLK), BLK), :]
        kept[part, 0:BLK] = here[:, :half]
        kept[part, BLK:2 * BLK] = here[:, half:]
        kept[part, 2 * BLK:] = tail
        here = block[pl.ds(pl.multiple_of((2 * part + 1 - core) * BLK, BLK), BLK), :].astype(jnp.bfloat16)
        sent[part, 0:BLK] = here[:, :half]
        sent[part, BLK:2 * BLK] = here[:, half:]
        sent[part, 2 * BLK:] = split_rows(tail)


def split_rows(tail):
    high = tail.astype(jnp.bfloat16)
    low = (tail - high.astype(jnp.float32)).astype(jnp.bfloat16)
    low = jnp.concatenate([low[-1:], low[:-1]], axis=0)
    row = lax.broadcasted_iota(jnp.int32, tail.shape, 0)
    return jnp.where(row % 2 == 0, high, low)


def add_kernel(kept, received, out):
    total = kept[...] + received[...].astype(jnp.float32)
    tail = total[0, 2 * BLK:]
    row = lax.broadcasted_iota(jnp.int32, tail.shape, 0)
    first, second = tail[0:1] + tail[1:2], tail[2:3] + tail[3:4]
    tail = split_rows(jnp.where(row == 0, first, jnp.where(row == 2, second, 0.0)))
    for part in range(out.shape[0]):
        out[part, 0:2 * BLK] = total[part, 0:2 * BLK].astype(jnp.bfloat16)
        out[part, 2 * BLK:] = tail


def final_kernel(parts, gram, rhs, *, factor):
    total = parts[0].astype(jnp.float32)
    for part in range(1, parts.shape[0]):
        total = total + parts[part].astype(jnp.float32)
    half = total.shape[1]
    gram[:, :half] = total[0:BLK] * factor
    gram[:, half:] = total[BLK:2 * BLK] * factor
    tail = 2 * BLK
    rhs[:, :half] = (total[tail:tail + 1] + total[tail + 1:tail + 2]) * factor
    rhs[:, half:] = (total[tail + 2:tail + 3] + total[tail + 3:tail + 4]) * factor


def per_device(features, environments, projector, metric, neighbours, counts, target):
    f32, bf16 = jnp.float32, jnp.bfloat16
    slab, width = features.shape[0], environments.shape[0]
    planes, ys = lax.axis_size("env"), lax.axis_size("y")
    group, cores = lax.axis_size("x"), lax.axis_size("core")
    devices = ys * group * cores
    shape = jax.ShapeDtypeStruct

    metric_rows = metric.transpose(0, 2, 1, 3).reshape(slab, -1)
    target_column = target.reshape(slab, 1)

    partial = pl.pallas_call(
        project_kernel,
        out_shape=shape((planes, slab, width), bf16),
        in_specs=[ANY] * 4,
        out_specs=ANY,
        scratch_shapes=[
            pltpu.SMEM(counts.shape, jnp.int32),
            pltpu.VMEM(features.shape, bf16),
            pltpu.VMEM(environments.shape, bf16),
            pltpu.VMEM(projector.shape, bf16),
            pltpu.VMEM((planes, slab, width), bf16),
            pltpu.SemaphoreType.DMA((4,)),
            pltpu.SemaphoreType.DMA((planes,)),
        ],
        compiler_params=WHOLE,
    )(counts, features, environments, projector)
    partial = lax.all_to_all(partial, "env", 0, 0, tiled=True, axis_index_groups=[list(ORDER)])
    psi, turned = pl.pallas_call(
        sum_kernel,
        out_shape=(shape((slab, width), bf16), shape((group * planes, width // group, slab), bf16)),
        in_specs=[VMEM] * 3,
        out_specs=(VMEM, VMEM),
        compiler_params=PARAMS,
    )(partial, metric_rows, target_column)
    message = shape((slab + EXTRA, width), bf16)
    inner, own, outer = pl.pallas_call(
        spread_kernel,
        out_shape=(message, shape(message.shape, f32), message),
        in_specs=[SMEM] + [VMEM] * 3,
        out_specs=(VMEM,) * 3,
        scratch_shapes=[pltpu.VMEM((3 * slab, width + LANES), f32)],
        compiler_params=PARAMS,
    )(neighbours, psi, metric_rows, target_column)
    next_chip = [(i, i + 2 * (i % 2) - 1) for i in range(1, devices - 1)]
    outer = lax.ppermute(outer, ROWS_AXES, next_chip)
    inner = lax.ppermute(inner, "core", [(0, 1), (1, 0)])
    both = [part * planes + z for part in range(group) for z in ORDER]
    turned = lax.all_to_all(turned, ("x", "env"), 0, 0, tiled=True, axis_index_groups=[both])
    carried = pl.pallas_call(
        weighted_kernel,
        out_shape=shape((slab + EXTRA, width), bf16),
        in_specs=[VMEM] * 4,
        out_specs=VMEM,
        compiler_params=PARAMS,
    )(psi, own, inner, outer)
    shifted = [
        lax.ppermute(carried, "x", [(i, i ^ step) for i in range(group)]) for step in range(1, group)
    ]
    parts = (ys, 2 * BLK + EXTRA, width // 2)
    kept, sent = pl.pallas_call(
        gram_kernel,
        out_shape=(shape(parts, f32), shape(parts, bf16)),
        in_specs=[SMEM] + [VMEM] * (1 + group),
        out_specs=(VMEM, VMEM),
        scratch_shapes=[pltpu.VMEM((planes * width // group, width), f32)],
        compiler_params=PARAMS,
    )(neighbours, turned, carried, *shifted)
    received = lax.ppermute(sent, "core", [(0, 1), (1, 0)])
    terms = pl.pallas_call(
        add_kernel,
        out_shape=shape(parts, bf16),
        in_specs=[VMEM, VMEM],
        out_specs=VMEM,
        compiler_params=PARAMS,
    )(kept, received)
    terms = lax.all_to_all(terms, "y", 0, 0, tiled=True, axis_index_groups=[list(ORDER)])

    def finish(parts, gram, rhs):
        final_kernel(parts, gram, rhs, factor=1.0 / (slab * devices) ** 0.5)

    gram, rhs = pl.pallas_call(
        finish,
        out_shape=(shape((BLK, width), f32), shape((1, width), f32)),
        in_specs=[VMEM],
        out_specs=(VMEM, VMEM),
        compiler_params=PARAMS,
    )(terms)
    return gram, rhs.reshape(width)


def solution(mesh):
    ys, xs, cores = 8, 4, 2
    split = Mesh(mesh.devices.reshape(ys, xs, cores, mesh.shape["env"]), ("y", "x", "core", "env"))
    rows = P(ROWS_AXES)
    return jax.shard_map(
        per_device,
        mesh=split,
        in_specs=(
            P(ROWS_AXES, None),
            P("env", None),
            P("env", None),
            P(ROWS_AXES, None, None, None),
            P(ROWS_AXES, None),
            rows,
            rows,
        ),
        out_specs=(P(ROWS_AXES, "env"), P("env")),
        check_vma=False,
    )
```

```python
import jax
import jax.numpy as jnp
from jax import lax
from jax.experimental import pallas as pl
from jax.experimental.pallas import tpu as pltpu
from jax.sharding import Mesh, PartitionSpec as P

BLK = 32
EXTRA = 16
LANES = 128
STEPS = (1, 3, 2)
ROWS_AXES = ("y", "x", "core")
ORDER = (0, 2, 4, 6, 1, 3, 5, 7)
VMEM = pl.BlockSpec(memory_space=pltpu.VMEM)
SMEM = pl.BlockSpec(memory_space=pltpu.SMEM)
ANY = pl.BlockSpec(memory_space=pl.ANY)
PARAMS = pltpu.CompilerParams(vmem_limit_bytes=40 * 1024 * 1024)
WHOLE = pltpu.CompilerParams(vmem_limit_bytes=60 * 1024 * 1024)


def dot(a, b, dims):
    return lax.dot_general(a, b, (dims, ((), ())), preferred_element_type=jnp.float32)


def project_kernel(
    counts, features, environments, projector, out, slots_used, left, right, weights, parts, sems, sent
):
    copies = [
        pltpu.make_async_copy(source, target, sems.at[i])
        for i, (source, target) in enumerate(
            [(features, left), (environments, right), (counts, slots_used), (projector, weights)]
        )
    ]
    for copy in copies:
        copy.start()
    for copy in copies[:3]:
        copy.wait()
    kern = dot(left[...], right[...], ((1,), (1,)))
    kern = (kern * kern).astype(jnp.bfloat16)
    rows, width = kern.shape
    slots = lax.broadcasted_iota(jnp.int32, (BLK, width), 0)
    masked = jnp.concatenate(
        [
            jnp.where(slots < slots_used[b], kern[b * BLK:(b + 1) * BLK], jnp.bfloat16(0))
            for b in range(rows // BLK)
        ],
        axis=0,
    )
    copies[3].wait()
    for part in range(out.shape[0]):
        cols = slice(part * width, (part + 1) * width)
        parts[part] = dot(masked, weights[:, cols], ((1,), (0,))).astype(jnp.bfloat16)
        pltpu.make_async_copy(parts.at[part], out.at[ORDER.index(part)], sent.at[part]).start()
    for part in range(out.shape[0]):
        pltpu.make_async_copy(parts.at[part], out.at[ORDER.index(part)], sent.at[part]).wait()


def unit(size):
    row = lax.broadcasted_iota(jnp.int32, (size, size), 0)
    return (row == lax.broadcasted_iota(jnp.int32, (size, size), 1)).astype(jnp.bfloat16)


def sum_kernel(parts, metric, target, psi, out):
    del metric, target
    total = parts[0].astype(jnp.float32)
    for part in range(1, parts.shape[0]):
        total = total + parts[part].astype(jnp.float32)
    total = total.astype(jnp.bfloat16)
    psi[...] = total
    rows, width = total.shape
    turned = dot(total, unit(rows), ((0,), (0,))).astype(jnp.bfloat16)
    pieces, chunk = out.shape[0], out.shape[1]
    group = width // chunk
    planes = pieces // group
    for part in range(group):
        for z in range(planes):
            out[part * planes + z] = turned[part * chunk:(part + 1) * chunk, :]


def high_low(row, extra):
    high = row.astype(jnp.bfloat16)
    low = (row - high.astype(jnp.float32)).astype(jnp.bfloat16)
    line = lax.broadcasted_iota(jnp.int32, (extra, row.shape[1]), 0)
    return jnp.where(line == 0, high, jnp.where(line == 1, low, jnp.bfloat16(0)))


def spread_kernel(neighbours, psi, metric, target, inner, own, outer, cells):
    rows, width = psi.shape
    cells[...] = jnp.zeros_like(cells)
    first = neighbours[0, 0] - rows // BLK
    high = target[...].astype(jnp.bfloat16)
    low = (target[...] - high.astype(jnp.float32)).astype(jnp.bfloat16)
    lane = lax.broadcasted_iota(jnp.int32, (rows, LANES), 1)
    column = jnp.where(lane == 0, high, jnp.where(lane == 1, low, jnp.bfloat16(0)))
    wide = jnp.concatenate([psi[...], column], axis=1)
    for b in range(rows // BLK):
        here = slice(b * BLK, (b + 1) * BLK)
        terms = dot(metric[here, :], wide[here, :], ((0,), (0,)))
        for j in range(neighbours.shape[1]):
            there = pl.ds(pl.multiple_of((neighbours[b, j] - first) * BLK, BLK), BLK)
            cells[there, :] = cells[there, :] + terms[j * BLK:(j + 1) * BLK]
    core = neighbours[0, 0] // (rows // BLK) % 2
    for out, start in ((inner, 2 * rows * (1 - core)), (own, rows), (outer, 2 * rows * core)):
        block = cells[pl.ds(pl.multiple_of(start, rows), rows), :]
        weight = block[:, width:width + 1] + block[:, width + 1:width + 2]
        high = weight.astype(jnp.bfloat16)
        low = (weight - high.astype(jnp.float32)).astype(jnp.bfloat16)
        column = jnp.where(lane == 0, high, jnp.where(lane == 1, low, jnp.bfloat16(0)))
        out[0:rows] = block[:, :width].astype(out.dtype)
        out[rows:] = dot(column, unit(rows), ((0,), (0,)))[0:EXTRA].astype(out.dtype)


def weighted_kernel(psi, own, outer, inner, carried):
    rows, width = psi.shape
    total = own[0:rows] + inner[0:rows].astype(jnp.float32) + outer[0:rows].astype(jnp.float32)
    carried[0:rows] = total.astype(jnp.bfloat16)
    rhs = jnp.zeros((1, width), jnp.float32)
    for cells in (own, inner, outer):
        terms = dot(cells[rows:].astype(jnp.bfloat16), psi[...], ((1,), (0,)))
        rhs = rhs + (terms[0:1] + terms[1:2])
    carried[rows:] = high_low(rhs, carried.shape[0] - rows)


def gram_kernel(neighbours, pieces, own, *rest):
    carried, (kept, sent, block) = (own,) + rest[:-3], rest[-3:]
    group = len(carried)
    planes = pieces.shape[0] // group
    chunk, rows, width = pieces.shape[1], pieces.shape[2], own.shape[1]
    x = neighbours[0, 0] // (2 * (rows // BLK)) % group
    total = jnp.zeros((planes * chunk, width), jnp.float32)
    rhs = jnp.zeros((1, width), jnp.float32)
    for step, cells in zip((0,) + STEPS, carried):
        source = x ^ step
        turned = pieces[pl.ds(source * planes, planes)].reshape(planes * chunk, rows)
        total = total + dot(turned, cells[0:rows], ((1,), (0,)))
        tail = cells[rows:].astype(jnp.float32)
        rhs = rhs + (tail[0:1] + tail[1:2])
    lines = high_low(rhs, EXTRA)
    half = width // 2
    block[...] = total
    core = neighbours[0, 0] // (rows // BLK) % 2
    row = lax.broadcasted_iota(jnp.int32, (EXTRA, half), 0)
    tail = jnp.where(row == 0, rhs[:, :half], jnp.where(row == 2, rhs[:, half:], 0.0))
    for part in range(kept.shape[0]):
        here = block[pl.ds(pl.multiple_of((2 * part + core) * BLK, BLK), BLK), :]
        kept[part, 0:BLK] = here[:, :half]
        kept[part, BLK:2 * BLK] = here[:, half:]
        kept[part, 2 * BLK:] = tail
        here = block[pl.ds(pl.multiple_of((2 * part + 1 - core) * BLK, BLK), BLK), :].astype(jnp.bfloat16)
        sent[part, 0:BLK] = here[:, :half]
        sent[part, BLK:2 * BLK] = here[:, half:]
        sent[part, 2 * BLK:] = split_rows(tail)


def split_rows(tail):
    high = tail.astype(jnp.bfloat16)
    low = (tail - high.astype(jnp.float32)).astype(jnp.bfloat16)
    low = jnp.concatenate([low[-1:], low[:-1]], axis=0)
    row = lax.broadcasted_iota(jnp.int32, tail.shape, 0)
    return jnp.where(row % 2 == 0, high, low)


def add_kernel(kept, received, out):
    total = kept[...] + received[...].astype(jnp.float32)
    tail = total[0, 2 * BLK:]
    row = lax.broadcasted_iota(jnp.int32, tail.shape, 0)
    first, second = tail[0:1] + tail[1:2], tail[2:3] + tail[3:4]
    tail = split_rows(jnp.where(row == 0, first, jnp.where(row == 2, second, 0.0)))
    for part in range(out.shape[0]):
        out[part, 0:2 * BLK] = total[part, 0:2 * BLK].astype(jnp.bfloat16)
        out[part, 2 * BLK:] = tail


def final_kernel(parts, gram, rhs, *, factor):
    total = parts[0].astype(jnp.float32)
    for part in range(1, parts.shape[0]):
        total = total + parts[part].astype(jnp.float32)
    half = total.shape[1]
    gram[:, :half] = total[0:BLK] * factor
    gram[:, half:] = total[BLK:2 * BLK] * factor
    tail = 2 * BLK
    rhs[:, :half] = (total[tail:tail + 1] + total[tail + 1:tail + 2]) * factor
    rhs[:, half:] = (total[tail + 2:tail + 3] + total[tail + 3:tail + 4]) * factor


def per_device(features, environments, projector, metric, neighbours, counts, target):
    f32, bf16 = jnp.float32, jnp.bfloat16
    slab, width = features.shape[0], environments.shape[0]
    planes, ys = lax.axis_size("env"), lax.axis_size("y")
    group, cores = lax.axis_size("x"), lax.axis_size("core")
    devices = ys * group * cores
    shape = jax.ShapeDtypeStruct

    metric_rows = metric.transpose(0, 2, 1, 3).reshape(slab, -1)
    target_column = target.reshape(slab, 1)

    partial = pl.pallas_call(
        project_kernel,
        out_shape=shape((planes, slab, width), bf16),
        in_specs=[ANY] * 4,
        out_specs=ANY,
        scratch_shapes=[
            pltpu.SMEM(counts.shape, jnp.int32),
            pltpu.VMEM(features.shape, bf16),
            pltpu.VMEM(environments.shape, bf16),
            pltpu.VMEM(projector.shape, bf16),
            pltpu.VMEM((planes, slab, width), bf16),
            pltpu.SemaphoreType.DMA((4,)),
            pltpu.SemaphoreType.DMA((planes,)),
        ],
        compiler_params=WHOLE,
    )(counts, features, environments, projector)
    partial = lax.all_to_all(partial, "env", 0, 0, tiled=True, axis_index_groups=[list(ORDER)])
    psi, turned = pl.pallas_call(
        sum_kernel,
        out_shape=(shape((slab, width), bf16), shape((group * planes, width // group, slab), bf16)),
        in_specs=[VMEM] * 3,
        out_specs=(VMEM, VMEM),
        compiler_params=PARAMS,
    )(partial, metric_rows, target_column)
    message = shape((slab + EXTRA, width), bf16)
    inner, own, outer = pl.pallas_call(
        spread_kernel,
        out_shape=(message, shape(message.shape, f32), message),
        in_specs=[SMEM] + [VMEM] * 3,
        out_specs=(VMEM,) * 3,
        scratch_shapes=[pltpu.VMEM((3 * slab, width + LANES), f32)],
        compiler_params=PARAMS,
    )(neighbours, psi, metric_rows, target_column)
    next_chip = [(i, i + 2 * (i % 2) - 1) for i in range(1, devices - 1)]
    inner = lax.ppermute(inner, "core", [(0, 1), (1, 0)])
    outer = lax.ppermute(outer, ROWS_AXES, next_chip)
    both = [part * planes + z for part in range(group) for z in ORDER]
    turned = lax.all_to_all(turned, ("x", "env"), 0, 0, tiled=True, axis_index_groups=[both])
    carried = pl.pallas_call(
        weighted_kernel,
        out_shape=shape((slab + EXTRA, width), bf16),
        in_specs=[VMEM] * 4,
        out_specs=VMEM,
        compiler_params=PARAMS,
    )(psi, own, outer, inner)
    shifted = [
        lax.ppermute(carried, "x", [(i, i ^ step) for i in range(group)]) for step in STEPS
    ]
    parts = (ys, 2 * BLK + EXTRA, width // 2)
    kept, sent = pl.pallas_call(
        gram_kernel,
        out_shape=(shape(parts, f32), shape(parts, bf16)),
        in_specs=[SMEM] + [VMEM] * (1 + group),
        out_specs=(VMEM, VMEM),
        scratch_shapes=[pltpu.VMEM((planes * width // group, width), f32)],
        compiler_params=PARAMS,
    )(neighbours, turned, carried, *shifted)
    received = lax.ppermute(sent, "core", [(0, 1), (1, 0)])
    terms = pl.pallas_call(
        add_kernel,
        out_shape=shape(parts, bf16),
        in_specs=[VMEM, VMEM],
        out_specs=VMEM,
        compiler_params=PARAMS,
    )(kept, received)
    terms = lax.all_to_all(terms, "y", 0, 0, tiled=True, axis_index_groups=[list(ORDER)])

    def finish(parts, gram, rhs):
        final_kernel(parts, gram, rhs, factor=1.0 / (slab * devices) ** 0.5)

    gram, rhs = pl.pallas_call(
        finish,
        out_shape=(shape((BLK, width), f32), shape((1, width), f32)),
        in_specs=[VMEM],
        out_specs=(VMEM, VMEM),
        compiler_params=PARAMS,
    )(terms)
    return gram, rhs.reshape(width)


def solution(mesh):
    ys, xs, cores = 8, 4, 2
    split = Mesh(mesh.devices.reshape(ys, xs, cores, mesh.shape["env"]), ("y", "x", "core", "env"))
    rows = P(ROWS_AXES)
    return jax.shard_map(
        per_device,
        mesh=split,
        in_specs=(
            P(ROWS_AXES, None),
            P("env", None),
            P("env", None),
            P(ROWS_AXES, None, None, None),
            P(ROWS_AXES, None),
            rows,
            rows,
        ),
        out_specs=(P(ROWS_AXES, "env"), P("env")),
        check_vma=False,
    )
```

```python
import jax
import jax.numpy as jnp
from jax import lax
from jax.experimental import pallas as pl
from jax.experimental.pallas import tpu as pltpu
from jax.sharding import Mesh, PartitionSpec as P

BLK = 32
EXTRA = 16
LANES = 128
STEPS = (1, 3, 2)
ROWS_AXES = ("y", "x", "core")
ORDER = (0, 2, 4, 6, 1, 3, 5, 7)
FIRST = (0, 4, 1, 5, 2, 6, 3, 7)
VMEM = pl.BlockSpec(memory_space=pltpu.VMEM)
SMEM = pl.BlockSpec(memory_space=pltpu.SMEM)
ANY = pl.BlockSpec(memory_space=pl.ANY)
PARAMS = pltpu.CompilerParams(vmem_limit_bytes=40 * 1024 * 1024)
WHOLE = pltpu.CompilerParams(vmem_limit_bytes=60 * 1024 * 1024)


def dot(a, b, dims):
    return lax.dot_general(a, b, (dims, ((), ())), preferred_element_type=jnp.float32)


def project_kernel(
    counts, features, environments, projector, out, slots_used, left, right, weights, parts, sems, sent
):
    copies = [
        pltpu.make_async_copy(source, target, sems.at[i])
        for i, (source, target) in enumerate(
            [(features, left), (environments, right), (counts, slots_used), (projector, weights)]
        )
    ]
    for copy in copies:
        copy.start()
    for copy in copies[:3]:
        copy.wait()
    kern = dot(left[...], right[...], ((1,), (1,)))
    kern = (kern * kern).astype(jnp.bfloat16)
    rows, width = kern.shape
    slots = lax.broadcasted_iota(jnp.int32, (BLK, width), 0)
    masked = jnp.concatenate(
        [
            jnp.where(slots < slots_used[b], kern[b * BLK:(b + 1) * BLK], jnp.bfloat16(0))
            for b in range(rows // BLK)
        ],
        axis=0,
    )
    copies[3].wait()
    for part in range(out.shape[0]):
        cols = slice(part * width, (part + 1) * width)
        parts[part] = dot(masked, weights[:, cols], ((1,), (0,))).astype(jnp.bfloat16)
        pltpu.make_async_copy(parts.at[part], out.at[FIRST.index(part)], sent.at[part]).start()
    for part in range(out.shape[0]):
        pltpu.make_async_copy(parts.at[part], out.at[FIRST.index(part)], sent.at[part]).wait()


def unit(size):
    row = lax.broadcasted_iota(jnp.int32, (size, size), 0)
    return (row == lax.broadcasted_iota(jnp.int32, (size, size), 1)).astype(jnp.bfloat16)


def sum_kernel(parts, metric, target, psi, out):
    del metric, target
    total = parts[0].astype(jnp.float32)
    for part in range(1, parts.shape[0]):
        total = total + parts[part].astype(jnp.float32)
    total = total.astype(jnp.bfloat16)
    psi[...] = total
    rows, width = total.shape
    turned = dot(total, unit(rows), ((0,), (0,))).astype(jnp.bfloat16)
    pieces, chunk = out.shape[0], out.shape[1]
    group = width // chunk
    planes = pieces // group
    for part in range(group):
        for z in range(planes):
            out[part * planes + z] = turned[part * chunk:(part + 1) * chunk, :]


def high_low(row, extra):
    high = row.astype(jnp.bfloat16)
    low = (row - high.astype(jnp.float32)).astype(jnp.bfloat16)
    line = lax.broadcasted_iota(jnp.int32, (extra, row.shape[1]), 0)
    return jnp.where(line == 0, high, jnp.where(line == 1, low, jnp.bfloat16(0)))


def spread_kernel(neighbours, psi, metric, target, inner, own, outer, cells):
    rows, width = psi.shape
    cells[...] = jnp.zeros_like(cells)
    first = neighbours[0, 0] - rows // BLK
    high = target[...].astype(jnp.bfloat16)
    low = (target[...] - high.astype(jnp.float32)).astype(jnp.bfloat16)
    lane = lax.broadcasted_iota(jnp.int32, (rows, LANES), 1)
    column = jnp.where(lane == 0, high, jnp.where(lane == 1, low, jnp.bfloat16(0)))
    wide = jnp.concatenate([psi[...], column], axis=1)
    for b in range(rows // BLK):
        here = slice(b * BLK, (b + 1) * BLK)
        terms = dot(metric[here, :], wide[here, :], ((0,), (0,)))
        for j in range(neighbours.shape[1]):
            there = pl.ds(pl.multiple_of((neighbours[b, j] - first) * BLK, BLK), BLK)
            cells[there, :] = cells[there, :] + terms[j * BLK:(j + 1) * BLK]
    core = neighbours[0, 0] // (rows // BLK) % 2
    for out, start in ((inner, 2 * rows * (1 - core)), (own, rows), (outer, 2 * rows * core)):
        block = cells[pl.ds(pl.multiple_of(start, rows), rows), :]
        weight = block[:, width:width + 1] + block[:, width + 1:width + 2]
        high = weight.astype(jnp.bfloat16)
        low = (weight - high.astype(jnp.float32)).astype(jnp.bfloat16)
        column = jnp.where(lane == 0, high, jnp.where(lane == 1, low, jnp.bfloat16(0)))
        out[0:rows] = block[:, :width].astype(out.dtype)
        out[rows:] = dot(column, unit(rows), ((0,), (0,)))[0:EXTRA].astype(out.dtype)


def weighted_kernel(psi, own, outer, inner, carried):
    rows, width = psi.shape
    total = own[0:rows] + inner[0:rows].astype(jnp.float32) + outer[0:rows].astype(jnp.float32)
    carried[0:rows] = total.astype(jnp.bfloat16)
    rhs = jnp.zeros((1, width), jnp.float32)
    for cells in (own, inner, outer):
        terms = dot(cells[rows:].astype(jnp.bfloat16), psi[...], ((1,), (0,)))
        rhs = rhs + (terms[0:1] + terms[1:2])
    carried[rows:] = high_low(rhs, carried.shape[0] - rows)


def gram_kernel(neighbours, pieces, own, *rest):
    carried, (kept, sent, block) = (own,) + rest[:-3], rest[-3:]
    group = len(carried)
    planes = pieces.shape[0] // group
    chunk, rows, width = pieces.shape[1], pieces.shape[2], own.shape[1]
    x = neighbours[0, 0] // (2 * (rows // BLK)) % group
    total = jnp.zeros((planes * chunk, width), jnp.float32)
    rhs = jnp.zeros((1, width), jnp.float32)
    for step, cells in zip((0,) + STEPS, carried):
        source = x ^ step
        turned = pieces[pl.ds(source * planes, planes)].reshape(planes * chunk, rows)
        total = total + dot(turned, cells[0:rows], ((1,), (0,)))
        tail = cells[rows:].astype(jnp.float32)
        rhs = rhs + (tail[0:1] + tail[1:2])
    lines = high_low(rhs, EXTRA)
    half = width // 2
    block[...] = total
    core = neighbours[0, 0] // (rows // BLK) % 2
    row = lax.broadcasted_iota(jnp.int32, (EXTRA, half), 0)
    tail = jnp.where(row == 0, rhs[:, :half], jnp.where(row == 2, rhs[:, half:], 0.0))
    for part in range(kept.shape[0]):
        here = block[pl.ds(pl.multiple_of((2 * part + core) * BLK, BLK), BLK), :]
        kept[part, 0:BLK] = here[:, :half]
        kept[part, BLK:2 * BLK] = here[:, half:]
        kept[part, 2 * BLK:] = tail
        here = block[pl.ds(pl.multiple_of((2 * part + 1 - core) * BLK, BLK), BLK), :].astype(jnp.bfloat16)
        sent[part, 0:BLK] = here[:, :half]
        sent[part, BLK:2 * BLK] = here[:, half:]
        sent[part, 2 * BLK:] = split_rows(tail)


def split_rows(tail):
    high = tail.astype(jnp.bfloat16)
    low = (tail - high.astype(jnp.float32)).astype(jnp.bfloat16)
    low = jnp.concatenate([low[-1:], low[:-1]], axis=0)
    row = lax.broadcasted_iota(jnp.int32, tail.shape, 0)
    return jnp.where(row % 2 == 0, high, low)


def add_kernel(kept, received, out):
    total = kept[...] + received[...].astype(jnp.float32)
    tail = total[0, 2 * BLK:]
    row = lax.broadcasted_iota(jnp.int32, tail.shape, 0)
    first, second = tail[0:1] + tail[1:2], tail[2:3] + tail[3:4]
    tail = split_rows(jnp.where(row == 0, first, jnp.where(row == 2, second, 0.0)))
    for part in range(out.shape[0]):
        out[part, 0:2 * BLK] = total[part, 0:2 * BLK].astype(jnp.bfloat16)
        out[part, 2 * BLK:] = tail


def final_kernel(parts, gram, rhs, *, factor):
    total = parts[0].astype(jnp.float32)
    for part in range(1, parts.shape[0]):
        total = total + parts[part].astype(jnp.float32)
    half = total.shape[1]
    gram[:, :half] = total[0:BLK] * factor
    gram[:, half:] = total[BLK:2 * BLK] * factor
    tail = 2 * BLK
    rhs[:, :half] = (total[tail:tail + 1] + total[tail + 1:tail + 2]) * factor
    rhs[:, half:] = (total[tail + 2:tail + 3] + total[tail + 3:tail + 4]) * factor


def per_device(features, environments, projector, metric, neighbours, counts, target):
    f32, bf16 = jnp.float32, jnp.bfloat16
    slab, width = features.shape[0], environments.shape[0]
    planes, ys = lax.axis_size("env"), lax.axis_size("y")
    group, cores = lax.axis_size("x"), lax.axis_size("core")
    devices = ys * group * cores
    shape = jax.ShapeDtypeStruct

    metric_rows = metric.transpose(0, 2, 1, 3).reshape(slab, -1)
    target_column = target.reshape(slab, 1)

    partial = pl.pallas_call(
        project_kernel,
        out_shape=shape((planes, slab, width), bf16),
        in_specs=[ANY] * 4,
        out_specs=ANY,
        scratch_shapes=[
            pltpu.SMEM(counts.shape, jnp.int32),
            pltpu.VMEM(features.shape, bf16),
            pltpu.VMEM(environments.shape, bf16),
            pltpu.VMEM(projector.shape, bf16),
            pltpu.VMEM((planes, slab, width), bf16),
            pltpu.SemaphoreType.DMA((4,)),
            pltpu.SemaphoreType.DMA((planes,)),
        ],
        compiler_params=WHOLE,
    )(counts, features, environments, projector)
    partial = lax.all_to_all(partial, "env", 0, 0, tiled=True, axis_index_groups=[list(FIRST)])
    psi, turned = pl.pallas_call(
        sum_kernel,
        out_shape=(shape((slab, width), bf16), shape((group * planes, width // group, slab), bf16)),
        in_specs=[VMEM] * 3,
        out_specs=(VMEM, VMEM),
        compiler_params=PARAMS,
    )(partial, metric_rows, target_column)
    message = shape((slab + EXTRA, width), bf16)
    inner, own, outer = pl.pallas_call(
        spread_kernel,
        out_shape=(message, shape(message.shape, f32), message),
        in_specs=[SMEM] + [VMEM] * 3,
        out_specs=(VMEM,) * 3,
        scratch_shapes=[pltpu.VMEM((3 * slab, width + LANES), f32)],
        compiler_params=PARAMS,
    )(neighbours, psi, metric_rows, target_column)
    next_chip = [(i, i + 2 * (i % 2) - 1) for i in range(1, devices - 1)]
    inner = lax.ppermute(inner, "core", [(0, 1), (1, 0)])
    outer = lax.ppermute(outer, ROWS_AXES, next_chip)
    both = [part * planes + z for part in range(group) for z in ORDER]
    turned = lax.all_to_all(turned, ("x", "env"), 0, 0, tiled=True, axis_index_groups=[both])
    carried = pl.pallas_call(
        weighted_kernel,
        out_shape=shape((slab + EXTRA, width), bf16),
        in_specs=[VMEM] * 4,
        out_specs=VMEM,
        compiler_params=PARAMS,
    )(psi, own, outer, inner)
    shifted = [
        lax.ppermute(carried, "x", [(i, i ^ step) for i in range(group)]) for step in STEPS
    ]
    parts = (ys, 2 * BLK + EXTRA, width // 2)
    kept, sent = pl.pallas_call(
        gram_kernel,
        out_shape=(shape(parts, f32), shape(parts, bf16)),
        in_specs=[SMEM] + [VMEM] * (1 + group),
        out_specs=(VMEM, VMEM),
        scratch_shapes=[pltpu.VMEM((planes * width // group, width), f32)],
        compiler_params=PARAMS,
    )(neighbours, turned, carried, *shifted)
    received = lax.ppermute(sent, "core", [(0, 1), (1, 0)])
    terms = pl.pallas_call(
        add_kernel,
        out_shape=shape(parts, bf16),
        in_specs=[VMEM, VMEM],
        out_specs=VMEM,
        compiler_params=PARAMS,
    )(kept, received)
    terms = lax.all_to_all(terms, "y", 0, 0, tiled=True, axis_index_groups=[list(ORDER)])

    def finish(parts, gram, rhs):
        final_kernel(parts, gram, rhs, factor=1.0 / (slab * devices) ** 0.5)

    gram, rhs = pl.pallas_call(
        finish,
        out_shape=(shape((BLK, width), f32), shape((1, width), f32)),
        in_specs=[VMEM],
        out_specs=(VMEM, VMEM),
        compiler_params=PARAMS,
    )(terms)
    return gram, rhs.reshape(width)


def solution(mesh):
    ys, xs, cores = 8, 4, 2
    split = Mesh(mesh.devices.reshape(ys, xs, cores, mesh.shape["env"]), ("y", "x", "core", "env"))
    rows = P(ROWS_AXES)
    return jax.shard_map(
        per_device,
        mesh=split,
        in_specs=(
            P(ROWS_AXES, None),
            P("env", None),
            P("env", None),
            P(ROWS_AXES, None, None, None),
            P(ROWS_AXES, None),
            rows,
            rows,
        ),
        out_specs=(P(ROWS_AXES, "env"), P("env")),
        check_vma=False,
    )
```

```python
import jax
import jax.numpy as jnp
from jax import lax
from jax.experimental import pallas as pl
from jax.experimental.pallas import tpu as pltpu
from jax.sharding import Mesh, PartitionSpec as P

BLK = 32
EXTRA = 16
LANES = 128
STEPS = (1, 3, 2)
ROWS_AXES = ("y", "x", "core")
ORDER = (0, 2, 4, 6, 1, 3, 5, 7)
FIRST = (0, 4, 1, 5, 2, 6, 3, 7)
VMEM = pl.BlockSpec(memory_space=pltpu.VMEM)
SMEM = pl.BlockSpec(memory_space=pltpu.SMEM)
ANY = pl.BlockSpec(memory_space=pl.ANY)
PARAMS = pltpu.CompilerParams(vmem_limit_bytes=40 * 1024 * 1024)
WHOLE = pltpu.CompilerParams(vmem_limit_bytes=60 * 1024 * 1024)


def dot(a, b, dims):
    return lax.dot_general(a, b, (dims, ((), ())), preferred_element_type=jnp.float32)


def project_kernel(
    counts, features, environments, projector, out, slots_used, left, right, weights, parts, sems, sent
):
    copies = [
        pltpu.make_async_copy(source, target, sems.at[i])
        for i, (source, target) in enumerate(
            [(features, left), (environments, right), (counts, slots_used), (projector, weights)]
        )
    ]
    for copy in copies:
        copy.start()
    for copy in copies[:3]:
        copy.wait()
    kern = dot(left[...], right[...], ((1,), (1,)))
    kern = (kern * kern).astype(jnp.bfloat16)
    rows, width = kern.shape
    slots = lax.broadcasted_iota(jnp.int32, (BLK, width), 0)
    masked = jnp.concatenate(
        [
            jnp.where(slots < slots_used[b], kern[b * BLK:(b + 1) * BLK], jnp.bfloat16(0))
            for b in range(rows // BLK)
        ],
        axis=0,
    )
    copies[3].wait()
    for part in range(out.shape[0]):
        cols = slice(part * width, (part + 1) * width)
        parts[part] = dot(masked, weights[:, cols], ((1,), (0,))).astype(jnp.bfloat16)
        pltpu.make_async_copy(parts.at[part], out.at[FIRST.index(part)], sent.at[part]).start()
    for part in range(out.shape[0]):
        pltpu.make_async_copy(parts.at[part], out.at[FIRST.index(part)], sent.at[part]).wait()


def unit(size):
    row = lax.broadcasted_iota(jnp.int32, (size, size), 0)
    return (row == lax.broadcasted_iota(jnp.int32, (size, size), 1)).astype(jnp.bfloat16)


def sum_kernel(parts, metric, target, psi, out):
    del metric, target
    total = parts[0].astype(jnp.float32)
    for part in range(1, parts.shape[0]):
        total = total + parts[part].astype(jnp.float32)
    total = total.astype(jnp.bfloat16)
    psi[...] = total
    rows, width = total.shape
    turned = dot(total, unit(rows), ((0,), (0,))).astype(jnp.bfloat16)
    pieces, chunk = out.shape[0], out.shape[1]
    group = width // chunk
    planes = pieces // group
    for part in range(group):
        for z in range(planes):
            out[part * planes + z] = turned[part * chunk:(part + 1) * chunk, :]


def high_low(row, extra):
    high = row.astype(jnp.bfloat16)
    low = (row - high.astype(jnp.float32)).astype(jnp.bfloat16)
    line = lax.broadcasted_iota(jnp.int32, (extra, row.shape[1]), 0)
    return jnp.where(line == 0, high, jnp.where(line == 1, low, jnp.bfloat16(0)))


def spread_kernel(neighbours, psi, metric, target, inner, own, outer, cells):
    rows, width = psi.shape
    cells[...] = jnp.zeros_like(cells)
    first = neighbours[0, 0] - rows // BLK
    high = target[...].astype(jnp.bfloat16)
    low = (target[...] - high.astype(jnp.float32)).astype(jnp.bfloat16)
    lane = lax.broadcasted_iota(jnp.int32, (rows, LANES), 1)
    column = jnp.where(lane == 0, high, jnp.where(lane == 1, low, jnp.bfloat16(0)))
    wide = jnp.concatenate([psi[...], column], axis=1)
    for b in range(rows // BLK):
        here = slice(b * BLK, (b + 1) * BLK)
        terms = dot(metric[here, :], wide[here, :], ((0,), (0,)))
        for j in range(neighbours.shape[1]):
            there = pl.ds(pl.multiple_of((neighbours[b, j] - first) * BLK, BLK), BLK)
            cells[there, :] = cells[there, :] + terms[j * BLK:(j + 1) * BLK]
    core = neighbours[0, 0] // (rows // BLK) % 2
    for out, start in ((inner, 2 * rows * (1 - core)), (own, rows), (outer, 2 * rows * core)):
        block = cells[pl.ds(pl.multiple_of(start, rows), rows), :]
        weight = block[:, width:width + 1] + block[:, width + 1:width + 2]
        high = weight.astype(jnp.bfloat16)
        low = (weight - high.astype(jnp.float32)).astype(jnp.bfloat16)
        column = jnp.where(lane == 0, high, jnp.where(lane == 1, low, jnp.bfloat16(0)))
        out[0:rows] = block[:, :width].astype(out.dtype)
        out[rows:] = dot(column, unit(rows), ((0,), (0,)))[0:EXTRA].astype(out.dtype)


def weighted_kernel(psi, own, outer, inner, carried):
    rows, width = psi.shape
    total = own[0:rows] + inner[0:rows].astype(jnp.float32) + outer[0:rows].astype(jnp.float32)
    carried[0:rows] = total.astype(jnp.bfloat16)
    rhs = jnp.zeros((1, width), jnp.float32)
    for cells in (own, inner, outer):
        terms = dot(cells[rows:].astype(jnp.bfloat16), psi[...], ((1,), (0,)))
        rhs = rhs + (terms[0:1] + terms[1:2])
    carried[rows:] = high_low(rhs, carried.shape[0] - rows)


def gram_kernel(neighbours, pieces, own, *rest):
    carried, (kept, sent, block) = (own,) + rest[:-3], rest[-3:]
    group = len(carried)
    planes = pieces.shape[0] // group
    chunk, rows, width = pieces.shape[1], pieces.shape[2], own.shape[1]
    x = neighbours[0, 0] // (2 * (rows // BLK)) % group
    total = jnp.zeros((planes * chunk, width), jnp.float32)
    rhs = jnp.zeros((1, width), jnp.float32)
    for step, cells in zip((0,) + STEPS, carried):
        source = x ^ step
        turned = pieces[pl.ds(source * planes, planes)].reshape(planes * chunk, rows)
        total = total + dot(turned, cells[0:rows], ((1,), (0,)))
        tail = cells[rows:].astype(jnp.float32)
        rhs = rhs + (tail[0:1] + tail[1:2])
    lines = high_low(rhs, EXTRA)
    half = width // 2
    block[...] = total
    core = neighbours[0, 0] // (rows // BLK) % 2
    row = lax.broadcasted_iota(jnp.int32, (EXTRA, half), 0)
    tail = jnp.where(row == 0, rhs[:, :half], jnp.where(row == 2, rhs[:, half:], 0.0))
    for part in range(kept.shape[0]):
        place = FIRST.index(ORDER[part])
        here = block[pl.ds(pl.multiple_of((2 * part + core) * BLK, BLK), BLK), :]
        kept[place, 0:BLK] = here[:, :half]
        kept[place, BLK:2 * BLK] = here[:, half:]
        kept[place, 2 * BLK:] = tail
        here = block[pl.ds(pl.multiple_of((2 * part + 1 - core) * BLK, BLK), BLK), :].astype(jnp.bfloat16)
        sent[place, 0:BLK] = here[:, :half]
        sent[place, BLK:2 * BLK] = here[:, half:]
        sent[place, 2 * BLK:] = split_rows(tail)


def split_rows(tail):
    high = tail.astype(jnp.bfloat16)
    low = (tail - high.astype(jnp.float32)).astype(jnp.bfloat16)
    low = jnp.concatenate([low[-1:], low[:-1]], axis=0)
    row = lax.broadcasted_iota(jnp.int32, tail.shape, 0)
    return jnp.where(row % 2 == 0, high, low)


def add_kernel(kept, received, out):
    total = kept[...] + received[...].astype(jnp.float32)
    tail = total[0, 2 * BLK:]
    row = lax.broadcasted_iota(jnp.int32, tail.shape, 0)
    first, second = tail[0:1] + tail[1:2], tail[2:3] + tail[3:4]
    tail = split_rows(jnp.where(row == 0, first, jnp.where(row == 2, second, 0.0)))
    for part in range(out.shape[0]):
        out[part, 0:2 * BLK] = total[part, 0:2 * BLK].astype(jnp.bfloat16)
        out[part, 2 * BLK:] = tail


def final_kernel(parts, gram, rhs, *, factor):
    total = parts[0].astype(jnp.float32)
    for part in range(1, parts.shape[0]):
        total = total + parts[part].astype(jnp.float32)
    half = total.shape[1]
    gram[:, :half] = total[0:BLK] * factor
    gram[:, half:] = total[BLK:2 * BLK] * factor
    tail = 2 * BLK
    rhs[:, :half] = (total[tail:tail + 1] + total[tail + 1:tail + 2]) * factor
    rhs[:, half:] = (total[tail + 2:tail + 3] + total[tail + 3:tail + 4]) * factor


def per_device(features, environments, projector, metric, neighbours, counts, target):
    f32, bf16 = jnp.float32, jnp.bfloat16
    slab, width = features.shape[0], environments.shape[0]
    planes, ys = lax.axis_size("env"), lax.axis_size("y")
    group, cores = lax.axis_size("x"), lax.axis_size("core")
    devices = ys * group * cores
    shape = jax.ShapeDtypeStruct

    metric_rows = metric.transpose(0, 2, 1, 3).reshape(slab, -1)
    target_column = target.reshape(slab, 1)

    partial = pl.pallas_call(
        project_kernel,
        out_shape=shape((planes, slab, width), bf16),
        in_specs=[ANY] * 4,
        out_specs=ANY,
        scratch_shapes=[
            pltpu.SMEM(counts.shape, jnp.int32),
            pltpu.VMEM(features.shape, bf16),
            pltpu.VMEM(environments.shape, bf16),
            pltpu.VMEM(projector.shape, bf16),
            pltpu.VMEM((planes, slab, width), bf16),
            pltpu.SemaphoreType.DMA((4,)),
            pltpu.SemaphoreType.DMA((planes,)),
        ],
        compiler_params=WHOLE,
    )(counts, features, environments, projector)
    partial = lax.all_to_all(partial, "env", 0, 0, tiled=True, axis_index_groups=[list(FIRST)])
    psi, turned = pl.pallas_call(
        sum_kernel,
        out_shape=(shape((slab, width), bf16), shape((group * planes, width // group, slab), bf16)),
        in_specs=[VMEM] * 3,
        out_specs=(VMEM, VMEM),
        compiler_params=PARAMS,
    )(partial, metric_rows, target_column)
    message = shape((slab + EXTRA, width), bf16)
    inner, own, outer = pl.pallas_call(
        spread_kernel,
        out_shape=(message, shape(message.shape, f32), message),
        in_specs=[SMEM] + [VMEM] * 3,
        out_specs=(VMEM,) * 3,
        scratch_shapes=[pltpu.VMEM((3 * slab, width + LANES), f32)],
        compiler_params=PARAMS,
    )(neighbours, psi, metric_rows, target_column)
    next_chip = [(i, i + 2 * (i % 2) - 1) for i in range(1, devices - 1)]
    inner = lax.ppermute(inner, "core", [(0, 1), (1, 0)])
    outer = lax.ppermute(outer, ROWS_AXES, next_chip)
    both = [part * planes + z for part in range(group) for z in ORDER]
    turned = lax.all_to_all(turned, ("x", "env"), 0, 0, tiled=True, axis_index_groups=[both])
    carried = pl.pallas_call(
        weighted_kernel,
        out_shape=shape((slab + EXTRA, width), bf16),
        in_specs=[VMEM] * 4,
        out_specs=VMEM,
        compiler_params=PARAMS,
    )(psi, own, outer, inner)
    shifted = [
        lax.ppermute(carried, "x", [(i, i ^ step) for i in range(group)]) for step in STEPS
    ]
    parts = (ys, 2 * BLK + EXTRA, width // 2)
    kept, sent = pl.pallas_call(
        gram_kernel,
        out_shape=(shape(parts, f32), shape(parts, bf16)),
        in_specs=[SMEM] + [VMEM] * (1 + group),
        out_specs=(VMEM, VMEM),
        scratch_shapes=[pltpu.VMEM((planes * width // group, width), f32)],
        compiler_params=PARAMS,
    )(neighbours, turned, carried, *shifted)
    received = lax.ppermute(sent, "core", [(0, 1), (1, 0)])
    terms = pl.pallas_call(
        add_kernel,
        out_shape=shape(parts, bf16),
        in_specs=[VMEM, VMEM],
        out_specs=VMEM,
        compiler_params=PARAMS,
    )(kept, received)
    terms = lax.all_to_all(terms, "y", 0, 0, tiled=True, axis_index_groups=[list(FIRST)])

    def finish(parts, gram, rhs):
        final_kernel(parts, gram, rhs, factor=1.0 / (slab * devices) ** 0.5)

    gram, rhs = pl.pallas_call(
        finish,
        out_shape=(shape((BLK, width), f32), shape((1, width), f32)),
        in_specs=[VMEM],
        out_specs=(VMEM, VMEM),
        compiler_params=PARAMS,
    )(terms)
    return gram, rhs.reshape(width)


def solution(mesh):
    ys, xs, cores = 8, 4, 2
    split = Mesh(mesh.devices.reshape(ys, xs, cores, mesh.shape["env"]), ("y", "x", "core", "env"))
    rows = P(ROWS_AXES)
    return jax.shard_map(
        per_device,
        mesh=split,
        in_specs=(
            P(ROWS_AXES, None),
            P("env", None),
            P("env", None),
            P(ROWS_AXES, None, None, None),
            P(ROWS_AXES, None),
            rows,
            rows,
        ),
        out_specs=(P(ROWS_AXES, "env"), P("env")),
        check_vma=False,
    )
```

```python
import jax
import jax.numpy as jnp
from jax import lax
from jax.experimental import pallas as pl
from jax.experimental.pallas import tpu as pltpu
from jax.sharding import Mesh, PartitionSpec as P

BLK = 32
EXTRA = 16
LANES = 128
STEPS = (1, 3, 2)
ROWS_AXES = ("y", "x", "core")
ORDER = (0, 2, 4, 6, 1, 3, 5, 7)
FIRST = (0, 4, 1, 5, 2, 6, 3, 7)
VMEM = pl.BlockSpec(memory_space=pltpu.VMEM)
SMEM = pl.BlockSpec(memory_space=pltpu.SMEM)
ANY = pl.BlockSpec(memory_space=pl.ANY)
PARAMS = pltpu.CompilerParams(vmem_limit_bytes=40 * 1024 * 1024)
WHOLE = pltpu.CompilerParams(vmem_limit_bytes=60 * 1024 * 1024)


def dot(a, b, dims):
    return lax.dot_general(a, b, (dims, ((), ())), preferred_element_type=jnp.float32)


def project_kernel(
    counts, features, environments, projector, out, slots_used, left, right, weights, parts, sems, sent
):
    copies = [
        pltpu.make_async_copy(source, target, sems.at[i])
        for i, (source, target) in enumerate(
            [(features, left), (environments, right), (counts, slots_used), (projector, weights)]
        )
    ]
    for copy in copies:
        copy.start()
    for copy in copies[:2]:
        copy.wait()
    kern = dot(left[...], right[...], ((1,), (1,)))
    kern = (kern * kern).astype(jnp.bfloat16)
    copies[2].wait()
    rows, width = kern.shape
    slots = lax.broadcasted_iota(jnp.int32, (BLK, width), 0)
    masked = jnp.concatenate(
        [
            jnp.where(slots < slots_used[b], kern[b * BLK:(b + 1) * BLK], jnp.bfloat16(0))
            for b in range(rows // BLK)
        ],
        axis=0,
    )
    copies[3].wait()
    for part in range(out.shape[0]):
        cols = slice(part * width, (part + 1) * width)
        parts[part] = dot(masked, weights[:, cols], ((1,), (0,))).astype(jnp.bfloat16)
        pltpu.make_async_copy(parts.at[part], out.at[FIRST.index(part)], sent.at[part]).start()
    for part in range(out.shape[0]):
        pltpu.make_async_copy(parts.at[part], out.at[FIRST.index(part)], sent.at[part]).wait()


def unit(size):
    row = lax.broadcasted_iota(jnp.int32, (size, size), 0)
    return (row == lax.broadcasted_iota(jnp.int32, (size, size), 1)).astype(jnp.bfloat16)


def sum_kernel(parts, metric, target, psi, out):
    del metric, target
    total = parts[0].astype(jnp.float32)
    for part in range(1, parts.shape[0]):
        total = total + parts[part].astype(jnp.float32)
    total = total.astype(jnp.bfloat16)
    psi[...] = total
    rows, width = total.shape
    turned = dot(total, unit(rows), ((0,), (0,))).astype(jnp.bfloat16)
    pieces, chunk = out.shape[0], out.shape[1]
    group = width // chunk
    planes = pieces // group
    for part in range(group):
        for z in range(planes):
            out[part * planes + z] = turned[part * chunk:(part + 1) * chunk, :]


def high_low(row, extra):
    high = row.astype(jnp.bfloat16)
    low = (row - high.astype(jnp.float32)).astype(jnp.bfloat16)
    line = lax.broadcasted_iota(jnp.int32, (extra, row.shape[1]), 0)
    return jnp.where(line == 0, high, jnp.where(line == 1, low, jnp.bfloat16(0)))


def spread_kernel(neighbours, psi, metric, target, inner, own, outer, cells):
    rows, width = psi.shape
    cells[...] = jnp.zeros_like(cells)
    first = neighbours[0, 0] - rows // BLK
    high = target[...].astype(jnp.bfloat16)
    low = (target[...] - high.astype(jnp.float32)).astype(jnp.bfloat16)
    lane = lax.broadcasted_iota(jnp.int32, (rows, LANES), 1)
    column = jnp.where(lane == 0, high, jnp.where(lane == 1, low, jnp.bfloat16(0)))
    wide = jnp.concatenate([psi[...], column], axis=1)
    for b in range(rows // BLK):
        here = slice(b * BLK, (b + 1) * BLK)
        terms = dot(metric[here, :], wide[here, :], ((0,), (0,)))
        for j in range(neighbours.shape[1]):
            there = pl.ds(pl.multiple_of((neighbours[b, j] - first) * BLK, BLK), BLK)
            cells[there, :] = cells[there, :] + terms[j * BLK:(j + 1) * BLK]
    core = neighbours[0, 0] // (rows // BLK) % 2
    for out, start in ((inner, 2 * rows * (1 - core)), (own, rows), (outer, 2 * rows * core)):
        block = cells[pl.ds(pl.multiple_of(start, rows), rows), :]
        weight = block[:, width:width + 1] + block[:, width + 1:width + 2]
        high = weight.astype(jnp.bfloat16)
        low = (weight - high.astype(jnp.float32)).astype(jnp.bfloat16)
        column = jnp.where(lane == 0, high, jnp.where(lane == 1, low, jnp.bfloat16(0)))
        out[0:rows] = block[:, :width].astype(out.dtype)
        out[rows:] = dot(column, unit(rows), ((0,), (0,)))[0:EXTRA].astype(out.dtype)


def weighted_kernel(psi, own, outer, inner, carried):
    rows, width = psi.shape
    total = own[0:rows] + inner[0:rows].astype(jnp.float32) + outer[0:rows].astype(jnp.float32)
    carried[0:rows] = total.astype(jnp.bfloat16)
    rhs = jnp.zeros((1, width), jnp.float32)
    for cells in (own, inner, outer):
        terms = dot(cells[rows:].astype(jnp.bfloat16), psi[...], ((1,), (0,)))
        rhs = rhs + (terms[0:1] + terms[1:2])
    carried[rows:] = high_low(rhs, carried.shape[0] - rows)


def gram_kernel(neighbours, pieces, own, *rest):
    carried, (kept, sent, block) = (own,) + rest[:-3], rest[-3:]
    group = len(carried)
    planes = pieces.shape[0] // group
    chunk, rows, width = pieces.shape[1], pieces.shape[2], own.shape[1]
    x = neighbours[0, 0] // (2 * (rows // BLK)) % group
    total = jnp.zeros((planes * chunk, width), jnp.float32)
    rhs = jnp.zeros((1, width), jnp.float32)
    for step, cells in zip((0,) + STEPS, carried):
        source = x ^ step
        turned = pieces[pl.ds(source * planes, planes)].reshape(planes * chunk, rows)
        total = total + dot(turned, cells[0:rows], ((1,), (0,)))
        tail = cells[rows:].astype(jnp.float32)
        rhs = rhs + (tail[0:1] + tail[1:2])
    lines = high_low(rhs, EXTRA)
    half = width // 2
    block[...] = total
    core = neighbours[0, 0] // (rows // BLK) % 2
    row = lax.broadcasted_iota(jnp.int32, (EXTRA, half), 0)
    tail = jnp.where(row == 0, rhs[:, :half], jnp.where(row == 2, rhs[:, half:], 0.0))
    for part in range(kept.shape[0]):
        here = block[pl.ds(pl.multiple_of((2 * part + core) * BLK, BLK), BLK), :]
        kept[part, 0:BLK] = here[:, :half]
        kept[part, BLK:2 * BLK] = here[:, half:]
        kept[part, 2 * BLK:] = tail
        here = block[pl.ds(pl.multiple_of((2 * part + 1 - core) * BLK, BLK), BLK), :].astype(jnp.bfloat16)
        sent[part, 0:BLK] = here[:, :half]
        sent[part, BLK:2 * BLK] = here[:, half:]
        sent[part, 2 * BLK:] = split_rows(tail)


def split_rows(tail):
    high = tail.astype(jnp.bfloat16)
    low = (tail - high.astype(jnp.float32)).astype(jnp.bfloat16)
    low = jnp.concatenate([low[-1:], low[:-1]], axis=0)
    row = lax.broadcasted_iota(jnp.int32, tail.shape, 0)
    return jnp.where(row % 2 == 0, high, low)


def add_kernel(kept, received, out):
    total = kept[...] + received[...].astype(jnp.float32)
    tail = total[0, 2 * BLK:]
    row = lax.broadcasted_iota(jnp.int32, tail.shape, 0)
    first, second = tail[0:1] + tail[1:2], tail[2:3] + tail[3:4]
    tail = split_rows(jnp.where(row == 0, first, jnp.where(row == 2, second, 0.0)))
    for part in range(out.shape[0]):
        out[part, 0:2 * BLK] = total[part, 0:2 * BLK].astype(jnp.bfloat16)
        out[part, 2 * BLK:] = tail


def final_kernel(parts, gram, rhs, *, factor):
    total = parts[0].astype(jnp.float32)
    for part in range(1, parts.shape[0]):
        total = total + parts[part].astype(jnp.float32)
    half = total.shape[1]
    gram[:, :half] = total[0:BLK] * factor
    gram[:, half:] = total[BLK:2 * BLK] * factor
    tail = 2 * BLK
    rhs[:, :half] = (total[tail:tail + 1] + total[tail + 1:tail + 2]) * factor
    rhs[:, half:] = (total[tail + 2:tail + 3] + total[tail + 3:tail + 4]) * factor


def per_device(features, environments, projector, metric, neighbours, counts, target):
    f32, bf16 = jnp.float32, jnp.bfloat16
    slab, width = features.shape[0], environments.shape[0]
    planes, ys = lax.axis_size("env"), lax.axis_size("y")
    group, cores = lax.axis_size("x"), lax.axis_size("core")
    devices = ys * group * cores
    shape = jax.ShapeDtypeStruct

    metric_rows = metric.transpose(0, 2, 1, 3).reshape(slab, -1)
    target_column = target.reshape(slab, 1)

    partial = pl.pallas_call(
        project_kernel,
        out_shape=shape((planes, slab, width), bf16),
        in_specs=[ANY] * 4,
        out_specs=ANY,
        scratch_shapes=[
            pltpu.SMEM(counts.shape, jnp.int32),
            pltpu.VMEM(features.shape, bf16),
            pltpu.VMEM(environments.shape, bf16),
            pltpu.VMEM(projector.shape, bf16),
            pltpu.VMEM((planes, slab, width), bf16),
            pltpu.SemaphoreType.DMA((4,)),
            pltpu.SemaphoreType.DMA((planes,)),
        ],
        compiler_params=WHOLE,
    )(counts, features, environments, projector)
    partial = lax.all_to_all(partial, "env", 0, 0, tiled=True, axis_index_groups=[list(FIRST)])
    psi, turned = pl.pallas_call(
        sum_kernel,
        out_shape=(shape((slab, width), bf16), shape((group * planes, width // group, slab), bf16)),
        in_specs=[VMEM] * 3,
        out_specs=(VMEM, VMEM),
        compiler_params=PARAMS,
    )(partial, metric_rows, target_column)
    message = shape((slab + EXTRA, width), bf16)
    inner, own, outer = pl.pallas_call(
        spread_kernel,
        out_shape=(message, shape(message.shape, f32), message),
        in_specs=[SMEM] + [VMEM] * 3,
        out_specs=(VMEM,) * 3,
        scratch_shapes=[pltpu.VMEM((3 * slab, width + LANES), f32)],
        compiler_params=PARAMS,
    )(neighbours, psi, metric_rows, target_column)
    next_chip = [(i, i + 2 * (i % 2) - 1) for i in range(1, devices - 1)]
    inner = lax.ppermute(inner, "core", [(0, 1), (1, 0)])
    outer = lax.ppermute(outer, ROWS_AXES, next_chip)
    both = [part * planes + z for part in range(group) for z in ORDER]
    turned = lax.all_to_all(turned, ("x", "env"), 0, 0, tiled=True, axis_index_groups=[both])
    carried = pl.pallas_call(
        weighted_kernel,
        out_shape=shape((slab + EXTRA, width), bf16),
        in_specs=[VMEM] * 4,
        out_specs=VMEM,
        compiler_params=PARAMS,
    )(psi, own, outer, inner)
    shifted = [
        lax.ppermute(carried, "x", [(i, i ^ step) for i in range(group)]) for step in STEPS
    ]
    parts = (ys, 2 * BLK + EXTRA, width // 2)
    kept, sent = pl.pallas_call(
        gram_kernel,
        out_shape=(shape(parts, f32), shape(parts, bf16)),
        in_specs=[SMEM] + [VMEM] * (1 + group),
        out_specs=(VMEM, VMEM),
        scratch_shapes=[pltpu.VMEM((planes * width // group, width), f32)],
        compiler_params=PARAMS,
    )(neighbours, turned, carried, *shifted)
    received = lax.ppermute(sent, "core", [(0, 1), (1, 0)])
    terms = pl.pallas_call(
        add_kernel,
        out_shape=shape(parts, bf16),
        in_specs=[VMEM, VMEM],
        out_specs=VMEM,
        compiler_params=PARAMS,
    )(kept, received)
    terms = lax.all_to_all(terms, "y", 0, 0, tiled=True, axis_index_groups=[list(ORDER)])

    def finish(parts, gram, rhs):
        final_kernel(parts, gram, rhs, factor=1.0 / (slab * devices) ** 0.5)

    gram, rhs = pl.pallas_call(
        finish,
        out_shape=(shape((BLK, width), f32), shape((1, width), f32)),
        in_specs=[VMEM],
        out_specs=(VMEM, VMEM),
        compiler_params=PARAMS,
    )(terms)
    return gram, rhs.reshape(width)


def solution(mesh):
    ys, xs, cores = 8, 4, 2
    split = Mesh(mesh.devices.reshape(ys, xs, cores, mesh.shape["env"]), ("y", "x", "core", "env"))
    rows = P(ROWS_AXES)
    return jax.shard_map(
        per_device,
        mesh=split,
        in_specs=(
            P(ROWS_AXES, None),
            P("env", None),
            P("env", None),
            P(ROWS_AXES, None, None, None),
            P(ROWS_AXES, None),
            rows,
            rows,
        ),
        out_specs=(P(ROWS_AXES, "env"), P("env")),
        check_vma=False,
    )
```
